128 devices in a mesh: row: 16 (over y, x), col: 8 (over z, core).
Axes of the slice: x: 4, y: 4, z: 4, core: 2. Of those that a mesh axis runs over, the one named last changes fastest.
Arguments:
- features: bfloat16 [512, 384, 1024], P('row', 'col'), may hold values from -6 to 6
- conv_weight: bfloat16 [9216, 256], P(('row', 'col')), may hold values from -0.0625 to 0.0625
- conv_bias: float32 [256], replicated, may hold values from -3 to 3
- proj_weight: bfloat16 [256, 256], P(('row', 'col')), may hold values from -0.375 to 0.375
- cotangent: bfloat16 [512, 384, 256], P('row', 'col'), may hold values from -6 to 6
Outputs:
- projected: bfloat16 [512, 384, 256], P('row', 'col')
- features_grad: bfloat16 [512, 384, 1024], P('row', 'col')
- conv_weight_grad: float32 [9216, 256], P(('row', 'col'))
- proj_weight_grad: float32 [256, 256], P(('row', 'col'))
- bias_grad: float32 [256], P(('row', 'col'))
The draws below stay inside these ranges and needn't reach their ends.
All inputs are finite; a program needn't handle non-finite values.
Results may differ from the reference program's by a relative error of at most 0.015.
Values may be sent and summed in bfloat16 or wider, within the bound.
No kernel may reach another device: no remote copies, remote signals or barrier semaphores. Data moves between devices by JAX's collectives and lax.ppermute only.
A program may use at most 192 MiB of HBM per device.

```python
import jax
import jax.numpy as jnp
from jax import lax

CIN = 1024
C = 256
DILATION_RATE = 16
H = 512
W = 384


def raised(values, stream_key, source, target, blocks, factor):
    def block_of(dim):
        return (jnp.arange(values.shape[dim]) // (values.shape[dim] // blocks)).reshape((-1,) + (1,) * (values.ndim - 1 - dim))

    one_side = jax.random.permutation(stream_key, blocks)[block_of(target)]
    second = (block_of(target) + blocks // 2) % blocks
    return jnp.where((block_of(source) == one_side) | (block_of(source) == second), factor * values, values)


def shard_levels(own_key, dims, cuts, low, high):
    def one(dim, parts):
        steps = jax.random.uniform(jax.random.fold_in(jax.random.fold_in(own_key, 6), dim), (parts,), jnp.float32, low / len(cuts), high / len(cuts))
        return jnp.repeat(jnp.exp(steps), dims[dim] // parts).reshape((-1,) + (1,) * (len(dims) - dim - 1))

    factor_of = one(*cuts[0])
    for cut in cuts[1:]:
        factor_of = factor_of * one(*cut)
    return factor_of


def scatter_about(stream_key, shape, deviation, bound, cuts=(), dtype=jnp.bfloat16):
    entries = deviation * jax.random.normal(stream_key, shape, jnp.float32)
    if cuts:
        entries = entries * shard_levels(stream_key, shape, cuts, -0.22, 0.18)
    return jnp.clip(entries, -bound, bound).astype(dtype)


def noise_with(own_key, shape, spread, most, cuts, heavy, kind=jnp.bfloat16):
    entries = spread * jax.random.normal(own_key, shape, jnp.float32)
    if cuts:
        entries = entries * shard_levels(own_key, shape, cuts, -0.22, 0.18)
    return jnp.clip(raised(entries, jax.random.fold_in(own_key, 3), *heavy), -most, most).astype(kind)


def setup_inputs(seed: int = 0) -> dict:
    key_of = jax.random.split(jax.random.key(seed), 6)
    features = noise_with(key_of[0], (H, W, CIN), 1.0, 6.0, ((0, 16), (1, 8)), (0, 2, 16, 2.0))
    conv_weight = scatter_about(key_of[1], (9 * CIN, C), (9 * CIN) ** -0.5, 0.0625, ((0, 128),))
    conv_bias = scatter_about(key_of[2], (C,), 0.5, 3.0, (), jnp.float32)
    proj_weight = scatter_about(key_of[3], (C, C), C ** -0.5, 0.375, ((0, 128),))
    cotangent = scatter_about(key_of[4], (H, W, C), 1.0, 6.0, ((0, 16), (1, 8)))
    return {"features": features, "conv_weight": conv_weight, "conv_bias": conv_bias, "proj_weight": proj_weight, "cotangent": cotangent}


def window(padded_input, left_operand, right_operand, row_count, column_count):
    return padded_input[left_operand * DILATION_RATE:left_operand * DILATION_RATE + row_count, right_operand * DILATION_RATE:right_operand * DILATION_RATE + column_count]


def reference(features, conv_weight, conv_bias, proj_weight, cotangent):
    row_count, column_count, in_channels = features.shape
    out_channels = conv_bias.shape[0]
    pixels = row_count * column_count
    padded_input = jnp.pad(features, ((DILATION_RATE, DILATION_RATE), (DILATION_RATE, DILATION_RATE), (0, 0)))
    pre = jnp.zeros((pixels, out_channels), jnp.float32)
    for left_operand in range(3):
        for right_operand in range(3):
            tap = 3 * left_operand + right_operand
            piece = window(padded_input, left_operand, right_operand, row_count, column_count).reshape(pixels, in_channels)
            pre = pre + jnp.dot(piece, conv_weight[tap * in_channels:(tap + 1) * in_channels], preferred_element_type=jnp.float32)
    pre = pre + conv_bias[None, :]
    sig = jax.nn.sigmoid(pre)
    hidden = (pre * sig).astype(jnp.bfloat16)
    projected = jnp.dot(hidden, proj_weight, preferred_element_type=jnp.float32).astype(jnp.bfloat16)
    grad_flat = cotangent.reshape(pixels, out_channels)
    hidden_grad = lax.dot_general(grad_flat, proj_weight, (((1,), (1,)), ((), ())), preferred_element_type=jnp.float32)
    preactivation_gradient = (hidden_grad * sig * (1.0 + pre * (1.0 - sig))).astype(jnp.bfloat16)
    proj_weight_grad = lax.dot_general(hidden, grad_flat, (((0,), (0,)), ((), ())), preferred_element_type=jnp.float32)
    bias_grad = jnp.sum(preactivation_gradient.astype(jnp.float32), axis=0)
    padded_gradient = jnp.pad(preactivation_gradient.reshape(row_count, column_count, out_channels), ((DILATION_RATE, DILATION_RATE), (DILATION_RATE, DILATION_RATE), (0, 0)))
    blocks = []
    features_grad = jnp.zeros((pixels, in_channels), jnp.float32)
    for left_operand in range(3):
        for right_operand in range(3):
            tap = 3 * left_operand + right_operand
            block_weight = conv_weight[tap * in_channels:(tap + 1) * in_channels]
            piece = window(padded_input, left_operand, right_operand, row_count, column_count).reshape(pixels, in_channels)
            blocks.append(lax.dot_general(piece, preactivation_gradient, (((0,), (0,)), ((), ())), preferred_element_type=jnp.float32))
            back = window(padded_gradient, 2 - left_operand, 2 - right_operand, row_count, column_count).reshape(pixels, out_channels)
            features_grad = features_grad + lax.dot_general(back, block_weight, (((1,), (1,)), ((), ())), preferred_element_type=jnp.float32)
    conv_weight_grad = jnp.concatenate(blocks, axis=0)
    return (projected.reshape(row_count, column_count, out_channels), features_grad.astype(jnp.bfloat16).reshape(row_count, column_count, in_channels), conv_weight_grad, proj_weight_grad, bias_grad)
```

```python
import functools

import jax
import jax.numpy as jnp
import numpy as np
from jax import lax
from jax.experimental import pallas as pl
from jax.experimental.pallas import tpu as pltpu
from jax.sharding import Mesh, PartitionSpec as P

D = 16
CHIPS = ("y", "x", "z")
ALL = ("y", "x", "z", "core")
BF = jnp.bfloat16
F32 = jnp.float32
VMEM_LIMIT = 56 * 1024 * 1024

NN = (((1,), (0,)), ((), ()))
NT = (((1,), (1,)), ((), ()))


def dot(a, b, dims=NN):
    return lax.dot_general(a, b, dims, preferred_element_type=F32)


def vmem():
    return pl.BlockSpec(memory_space=pltpu.VMEM)


def hbm():
    return pl.BlockSpec(memory_space=pl.ANY)


def params():
    return pltpu.CompilerParams(vmem_limit_bytes=VMEM_LIMIT)


def cost(flops, size):
    return pl.CostEstimate(flops=flops, bytes_accessed=size, transcendentals=0)


def load_weights(core_ref, mine_ref, other_ref, w_ref, sems):
    core = core_ref[0]
    copies = []
    for k, (ref, half) in enumerate(((mine_ref, core), (other_ref, 1 - core))):
        lanes = pl.ds(pl.multiple_of(half * 128, 128), 128)
        copy = pltpu.make_async_copy(
            ref.at[:, pl.ds(0, 144), :], w_ref.at[:, :, lanes], sems.at[k]
        )
        copy.start()
        copies.append(copy)
    for copy in copies:
        copy.wait()
    return w_ref.reshape(9216, 256)


def tap(w, a, b):
    return w[(3 * a + b) * 1024 : (3 * a + b + 1) * 1024, :]


def px(ref, r0, r1, c0, c1):
    return ref[r0:r1, c0:c1, :].reshape((r1 - r0) * (c1 - c0), ref.shape[2])


def halo_kernel(core_ref, f_ref, mine_ref, other_ref, n_ref, s_ref, l_ref, r_ref, w_ref, acc, sems):
    w = load_weights(core_ref, mine_ref, other_ref, w_ref, sems)
    for out, a, r0, block in ((n_ref, 2, 0, 0), (s_ref, 0, 16, 3)):
        acc[...] = jnp.zeros_like(acc)
        for b in range(3):
            c = (2 - b) * D
            acc[:, c : c + 48, :] += dot(px(f_ref, r0, r0 + 16, 0, 48), tap(w, a, b)).reshape(16, 48, 256)
        l_ref[16 * block : 16 * block + 16] = acc[:, 0:16, :].astype(BF)
        out[...] = acc[:, 16:64, :].astype(BF)
        r_ref[16 * block : 16 * block + 16] = acc[:, 64:80, :].astype(BF)
    for out, b, c0 in ((l_ref, 2, 0), (r_ref, 0, 32)):
        mid = dot(px(f_ref, 0, 32, c0, c0 + 16), tap(w, 1, b))
        top = mid[:256] + dot(px(f_ref, 16, 32, c0, c0 + 16), tap(w, 2, b))
        low = mid[256:] + dot(px(f_ref, 0, 16, c0, c0 + 16), tap(w, 0, b))
        out[16:32] = top.reshape(16, 16, 256).astype(BF)
        out[32:48] = low.reshape(16, 16, 256).astype(BF)


def own_kernel(core_ref, f_ref, mine_ref, other_ref, cot_ref, proj_ref, bias_ref, pre_ref, hg_ref, w_ref, sems):
    w = load_weights(core_ref, mine_ref, other_ref, w_ref, sems)
    pre_ref[...] = (dot(px(f_ref, 0, 32, 0, 48), tap(w, 1, 1)) + bias_ref[...]).reshape(32, 48, 256)
    for a, rows in ((0, ((0, 16), (16, 32))), (1, ((0, 32), (0, 32))), (2, ((16, 32), (0, 16)))):
        for b, cols in ((0, ((0, 32), (16, 48))), (1, ((0, 48), (0, 48))), (2, ((16, 48), (0, 32)))):
            if a == 1 and b == 1:
                continue
            (fr, pr), (fc, pc) = rows, cols
            pre_ref[pr[0] : pr[1], pc[0] : pc[1], :] += dot(px(f_ref, *fr, *fc), tap(w, a, b)).reshape(
                pr[1] - pr[0], pc[1] - pc[0], 256
            )
    hg_ref[...] = dot(px(cot_ref, 0, 32, 0, 48), proj_ref[...], NT).reshape(32, 48, 256)


def point_kernel(core_ref, pre_ref, hg_ref, n_ref, s_ref, inner_ref, outer_ref, cn_ref, cs_ref, hid_ref, g_ref):
    core = core_ref[0]
    pre_ref[0:16] += n_ref[...].astype(F32)
    pre_ref[16:32] += s_ref[...].astype(F32)
    inner = pl.ds(pl.multiple_of(32 - 32 * core, 16), 16)
    outer = pl.ds(pl.multiple_of(32 * core, 16), 16)
    pre_ref[:, inner, :] += inner_ref[...].astype(F32)
    pre_ref[:, outer, :] += outer_ref[...].astype(F32)
    pre_ref[0:16, outer, :] += cn_ref[...].astype(F32)
    pre_ref[16:32, outer, :] += cs_ref[...].astype(F32)

    @pl.loop(0, 32)
    def _(r):
        pre = pre_ref[r]
        s = jax.nn.sigmoid(pre)
        hid_ref[r] = (pre * s).astype(BF)
        g_ref[r] = (hg_ref[r] * s * (1.0 + pre * (1.0 - s))).astype(BF)


def proj_kernel(hid_ref, cot_ref, proj_ref, g_ref, out_ref, pw_ref, bias_ref):
    hidden = px(hid_ref, 0, 32, 0, 48)
    out_ref[...] = dot(hidden, proj_ref[...]).astype(BF).reshape(32, 48, 256)
    pw_ref[...] = dot(hidden.T, px(cot_ref, 0, 32, 0, 48))
    bias_ref[...] = jnp.sum(px(g_ref, 0, 32, 0, 48).astype(F32), axis=0, keepdims=True)


def wgrad_kernel(core_ref, ft_ref, g_ref, mine_ref, other_ref):
    t = pl.program_id(0)
    row, col = (2 - t // 3) * D, (2 - t % 3) * D
    blocks = [
        g_ref[pl.ds(row + 16 * i, 16), pl.ds(pl.multiple_of(col + 16 * j, 16), 16), :].reshape(256, 256)
        for i in range(2)
        for j in range(3)
    ]
    res = dot(ft_ref[...], jnp.concatenate(blocks, axis=0))
    low, high = res[:, :128], res[:, 128:]
    first = core_ref[0] == 0
    mine_ref[...] = jnp.where(first, low, high).astype(BF)
    other_ref[...] = jnp.where(first, high, low).astype(BF)


def fgrad_kernel(core_ref, g_ref, mine_ref, other_ref, out_ref, w_ref, acc, sems):
    w = load_weights(core_ref, mine_ref, other_ref, w_ref, sems)
    acc[...] = jnp.zeros_like(acc)

    @pl.loop(0, 9)
    def _(t):
        row, col = (2 - t // 3) * D, (2 - t % 3) * D
        win = g_ref[pl.ds(row, 32), pl.ds(pl.multiple_of(col, 16), 48), :].reshape(1536, 256)
        acc[...] += dot(win, w[pl.ds(pl.multiple_of(t * 1024, 1024), 1024), :], NT)

    out_ref[...] = acc[...].astype(BF).reshape(32, 48, 1024)


def body(features, conv_weight, conv_bias, proj_weight, cotangent):
    core = lax.axis_index("core")
    is0 = core == 0
    core_s = core.astype(jnp.int32).reshape(1)
    smem = pl.BlockSpec(memory_space=pltpu.SMEM)

    def send(x, dr, dc):
        perm = []
        for i in range(128):
            r, c = i // 8, i % 8
            step = dc[c % 2]
            r2, c2 = r + dr, c + step
            if 0 <= r2 < 16 and 0 <= c2 < 8:
                perm.append((i, r2 * 8 + c2))
        return lax.ppermute(x, ALL, perm)

    SAME, INNER, OUTER = (0, 0), (1, -1), (-1, 1)

    shard = jnp.concatenate([conv_weight, proj_weight], axis=0)
    halves = jnp.where(is0, shard[:, 128:], shard[:, :128])
    keep = jnp.where(is0, shard[:, :128], shard[:, 128:])
    got = send(halves, 0, INNER)
    low, high = jnp.where(is0, keep, got), jnp.where(is0, got, keep)
    chunk = jnp.concatenate([low[:72], high[:72], low[72:], high[72:], jnp.zeros((4, 128), BF)], axis=0)
    mine = lax.all_to_all(jnp.broadcast_to(chunk[None], (64, 152, 128)), CHIPS, 0, 0)
    other = send(mine, 0, INNER)
    pm, po = mine[:, 144:148].reshape(256, 128), other[:, 144:148].reshape(256, 128)
    proj = jnp.concatenate([jnp.where(is0, pm, po), jnp.where(is0, po, pm)], axis=1)

    ft = features.reshape(2, 16, 3, 16, 1024).transpose(4, 0, 2, 1, 3).reshape(1024, 1536)

    wscratch = pltpu.VMEM((64, 144, 256), BF)
    tile_f32 = jax.ShapeDtypeStruct((32, 48, 256), F32)
    tile_bf = jax.ShapeDtypeStruct((32, 48, 256), BF)
    strip = jax.ShapeDtypeStruct((16, 48, 256), BF)
    side = jax.ShapeDtypeStruct((64, 16, 256), BF)

    n, s, l, r = pl.pallas_call(
        halo_kernel,
        out_shape=(strip, strip, side, side),
        in_specs=[smem, vmem(), hbm(), hbm()],
        out_specs=(vmem(),) * 4,
        scratch_shapes=[wscratch, pltpu.VMEM((16, 80, 256), F32), pltpu.SemaphoreType.DMA((2,))],
        compiler_params=params(),
        cost_estimate=cost(int(3.5e9), 9 << 20),
        name="halo",
    )(core_s, features, mine, other)
    inner_out, outer_out = jnp.where(is0, r, l), jnp.where(is0, l, r)
    inner = send(inner_out, 0, INNER)
    zero = jnp.zeros((16, 32, 256), BF)

    def widen(x):
        return jnp.where(is0, jnp.concatenate([zero, x], 1), jnp.concatenate([x, zero], 1))

    from_s = send(n + widen(inner[0:16]), -1, SAME)
    from_n = send(s + widen(inner[48:64]), 1, SAME)
    outer = send(outer_out[16:48], 0, OUTER)
    corner_s = send(outer_out[0:16], -1, OUTER)
    corner_n = send(outer_out[48:64], 1, OUTER)

    pre, hg = pl.pallas_call(
        own_kernel,
        out_shape=(tile_f32, tile_f32),
        in_specs=[smem, vmem(), hbm(), hbm(), vmem(), vmem(), vmem()],
        out_specs=(vmem(),) * 2,
        scratch_shapes=[wscratch, pltpu.SemaphoreType.DMA((2,))],
        compiler_params=params(),
        cost_estimate=cost(int(4.0e9), 12 << 20),
        name="own",
    )(core_s, features, mine, other, cotangent, proj, conv_bias.reshape(1, 256))

    hidden, g = pl.pallas_call(
        point_kernel,
        out_shape=(tile_bf, tile_bf),
        in_specs=[smem] + [vmem()] * 8,
        out_specs=(vmem(),) * 2,
        compiler_params=params(),
        cost_estimate=cost(int(1e8), 6 << 20),
        name="point",
    )(core_s, pre, hg, from_n, from_s, inner[16:48], outer, corner_n, corner_s)

    gl, gr = g[:, 0:16], g[:, 32:48]
    g_inner, g_outer = jnp.where(is0, gr, gl), jnp.where(is0, gl, gr)
    top = send(g[16:32], 1, SAME)
    bottom = send(g[0:16], -1, SAME)
    h_outer = send(g_outer, 0, OUTER)
    h_top = send(g_outer[16:32], 1, OUTER)
    h_bottom = send(g_outer[0:16], -1, OUTER)
    h_inner = send(g_inner, 0, INNER)
    edge = jnp.concatenate([top, bottom], axis=0)
    edge = jnp.where(is0, edge[:, 32:48], edge[:, 0:16])
    edge = send(edge, 0, INNER)

    projected, proj_term, bias_term = pl.pallas_call(
        proj_kernel,
        out_shape=(tile_bf, jax.ShapeDtypeStruct((256, 256), F32), jax.ShapeDtypeStruct((1, 256), F32)),
        in_specs=[vmem()] * 4,
        out_specs=(vmem(),) * 3,
        compiler_params=params(),
        cost_estimate=cost(int(4e8), 4 << 20),
        name="proj",
    )(hidden, cotangent, proj, g)

    outer_col = jnp.concatenate([h_top, h_outer, h_bottom], axis=0)
    inner_col = jnp.concatenate([edge[0:16], h_inner, edge[16:32]], axis=0)
    middle = jnp.concatenate([top, g, bottom], axis=0)
    gpad = jnp.concatenate(
        [jnp.where(is0, outer_col, inner_col), middle, jnp.where(is0, inner_col, outer_col)], axis=1
    )

    half = jax.ShapeDtypeStruct((9216, 128), BF)
    w_mine, w_other = pl.pallas_call(
        wgrad_kernel,
        grid=(9,),
        out_shape=(half, half),
        in_specs=[smem, vmem(), vmem()],
        out_specs=(pl.BlockSpec((1024, 128), lambda t: (t, 0)),) * 2,
        compiler_params=params(),
        cost_estimate=cost(int(7.2e9), 12 << 20),
        name="wgrad",
    )(core_s, ft, gpad)

    pl_, ph = proj_term[:, :128], proj_term[:, 128:]
    bias_rows = jnp.pad(bias_term.reshape(64, 1, 4), ((0, 0), (0, 3), (0, 124)))

    def with_proj(w, p):
        return jnp.concatenate([w.reshape(64, 144, 128), p.astype(BF).reshape(64, 4, 128), bias_rows.astype(BF)], 1)

    received = send(with_proj(w_other, jnp.where(is0, ph, pl_)), 0, INNER)
    total = with_proj(w_mine, jnp.where(is0, pl_, ph)).astype(F32) + received.astype(F32)
    pieces = lax.all_to_all(total.astype(BF), CHIPS, 0, 0)

    features_grad = pl.pallas_call(
        fgrad_kernel,
        out_shape=jax.ShapeDtypeStruct((32, 48, 1024), BF),
        in_specs=[smem, vmem(), hbm(), hbm()],
        out_specs=vmem(),
        scratch_shapes=[wscratch, pltpu.VMEM((1536, 1024), F32), pltpu.SemaphoreType.DMA((2,))],
        compiler_params=params(),
        cost_estimate=cost(int(7.2e9), 12 << 20),
        name="fgrad",
    )(core_s, gpad, mine, other)

    sums = jnp.sum(pieces.astype(F32), axis=0)
    lo, hi = jnp.concatenate([sums[:72], sums[144:146]], 0), jnp.concatenate([sums[72:144], sums[146:148]], 0)
    keep = jnp.where(is0, lo, hi)
    got = send(jnp.where(is0, hi, lo), 0, INNER)
    full = jnp.concatenate([jnp.where(is0, keep, got), jnp.where(is0, got, keep)], axis=1)
    bias_grad = jnp.where(is0, sums[148, 0:2], sums[148, 2:4])
    return projected, features_grad, full[:72], full[72:74], bias_grad


def solution(mesh):
    fine = Mesh(mesh.devices.reshape(4, 4, 4, 2), ALL)
    tile = P(("y", "x"), ("z", "core"), None)
    rows = P(ALL, None)
    return jax.shard_map(
        body,
        mesh=fine,
        in_specs=(tile, rows, P(), rows, tile),
        out_specs=(tile, tile, rows, rows, P(ALL)),
        check_vma=False,
    )
```

```python
import jax
import jax.numpy as jnp
import numpy as np
from jax import lax
from jax.experimental import pallas as pl
from jax.experimental.pallas import tpu as pltpu
from jax.sharding import Mesh, PartitionSpec as P

D = 16
CHIPS = ("y", "x", "z")
ALL = ("y", "x", "z", "core")
BF = jnp.bfloat16
F32 = jnp.float32
VMEM_LIMIT = 18 * 1024 * 1024

NN = (((1,), (0,)), ((), ()))
NT = (((1,), (1,)), ((), ()))
TN = (((0,), (0,)), ((), ()))


def dot(a, b, dims=NN):
    return lax.dot_general(a, b, dims, preferred_element_type=F32)


def vmem():
    return pl.BlockSpec(memory_space=pltpu.VMEM)


def params():
    return pltpu.CompilerParams(vmem_limit_bytes=VMEM_LIMIT)


def cost(flops, size):
    return pl.CostEstimate(flops=flops, bytes_accessed=size, transcendentals=0)


def swap(x):
    return jnp.concatenate([x[..., 128:], x[..., :128]], axis=-1)


def tap(mine_ref, other_ref, a, b):
    row = (3 * a + b) * 1024
    first, last = row // 144, -(-(row + 1024) // 144)
    skip = row - 144 * first

    def half(ref):
        return ref[first:last, 0:144, :].reshape((last - first) * 144, 128)[skip : skip + 1024]

    return jnp.concatenate([half(mine_ref), half(other_ref)], axis=1)


def px(ref, r0, r1, c0, c1):
    return ref[r0:r1, c0:c1, :].reshape((r1 - r0) * (c1 - c0), ref.shape[2])


def flip_kernel(f_ref, ft_ref):
    for k in range(6):
        i, j = divmod(k, 3)
        block = px(f_ref, 16 * i, 16 * i + 16, 16 * j, 16 * j + 16)
        ft_ref[:, 256 * k : 256 * k + 256] = block.T


def rows_kernel(core_ref, mine_ref, proj_ref, acc):
    for k in range(64):
        x = mine_ref[k, 144:152, :].astype(F32)
        acc[4 * k : 4 * k + 4, :128] = x[0:4]
        acc[4 * k : 4 * k + 4, 128:] = x[4:8]
    start = pl.multiple_of(128 * core_ref[0], 128)
    proj_ref[0:128] = acc[pl.ds(start, 128), :].astype(BF)
    proj_ref[128:256] = acc[pl.ds(128 - start, 128), :].astype(BF)


def halo_kernel(core_ref, f_ref, mine_ref, other_ref, n_ref, s_ref, inner_ref, outer_ref, cn_ref, cs_ref, sides, acc):
    core = core_ref[0]
    for out, a, r0, block in ((n_ref, 2, 0, 0), (s_ref, 0, 16, 3)):
        acc[...] = jnp.zeros_like(acc)
        for b in range(3):
            c = (2 - b) * D
            acc[:, c : c + 48, :] += dot(px(f_ref, r0, r0 + 16, 0, 48), tap(mine_ref, other_ref, a, b)).reshape(
                16, 48, 256
            )
        sides[0, 16 * block : 16 * block + 16] = acc[:, 0:16, :].astype(BF)
        out[...] = acc[:, 16:64, :].astype(BF)
        sides[1, 16 * block : 16 * block + 16] = acc[:, 64:80, :].astype(BF)
    for side, b, c0 in ((0, 2, 0), (1, 0, 32)):
        mid = dot(px(f_ref, 0, 32, c0, c0 + 16), tap(mine_ref, other_ref, 1, b))
        top = mid[:256] + dot(px(f_ref, 16, 32, c0, c0 + 16), tap(mine_ref, other_ref, 2, b))
        low = mid[256:] + dot(px(f_ref, 0, 16, c0, c0 + 16), tap(mine_ref, other_ref, 0, b))
        sides[side, 16:32] = top.reshape(16, 16, 256).astype(BF)
        sides[side, 32:48] = low.reshape(16, 16, 256).astype(BF)
    inner_ref[...] = sides[1 - core]
    outer_ref[...] = sides[core, 16:48]
    cn_ref[...] = sides[core, 0:16]
    cs_ref[...] = sides[core, 48:64]


def merge_kernel(core_ref, n_ref, s_ref, inner_ref, no_ref, so_ref):
    cols = pl.ds(pl.multiple_of(32 - 32 * core_ref[0], 16), 16)
    for src, dst, r in ((n_ref, no_ref, 0), (s_ref, so_ref, 48)):
        dst[...] = src[...]
        dst[:, cols, :] = (src[:, cols, :].astype(F32) + swap(inner_ref[r : r + 16]).astype(F32)).astype(BF)


def own_kernel(f_ref, mine_ref, other_ref, cot_ref, proj_ref, bias_ref, pre_ref, hg_ref):
    first = dot(px(f_ref, 0, 32, 0, 48), tap(mine_ref, other_ref, 1, 1))
    pre_ref[...] = (first + bias_ref[...]).reshape(32, 48, 256)
    for a, rows in ((0, ((0, 16), (16, 32))), (1, ((0, 32), (0, 32))), (2, ((16, 32), (0, 16)))):
        for b, cols in ((0, ((0, 32), (16, 48))), (1, ((0, 48), (0, 48))), (2, ((16, 48), (0, 32)))):
            if a == 1 and b == 1:
                continue
            (fr, pr), (fc, pc) = rows, cols
            pre_ref[pr[0] : pr[1], pc[0] : pc[1], :] += dot(
                px(f_ref, *fr, *fc), tap(mine_ref, other_ref, a, b)
            ).reshape(pr[1] - pr[0], pc[1] - pc[0], 256)
    hg_ref[...] = dot(px(cot_ref, 0, 32, 0, 48), proj_ref[...], NT).reshape(32, 48, 256)


def point_kernel(
    core_ref, own_ref, hg_ref, n_ref, s_ref, inner_ref, outer_ref, cn_ref, cs_ref,
    hid_ref, top_ref, low_ref, gi_ref, go_ref, ct_ref, cl_ref, pre_ref,
):
    core = core_ref[0]
    inner = pl.ds(pl.multiple_of(32 - 32 * core, 16), 16)
    outer = pl.ds(pl.multiple_of(32 * core, 16), 16)
    pre_ref[0:16] = own_ref[0:16] + n_ref[...].astype(F32)
    pre_ref[16:32] = own_ref[16:32] + s_ref[...].astype(F32)
    pre_ref[:, inner, :] += swap(inner_ref[16:48]).astype(F32)
    pre_ref[:, outer, :] += swap(outer_ref[...]).astype(F32)
    pre_ref[0:16, outer, :] += swap(cn_ref[...]).astype(F32)
    pre_ref[16:32, outer, :] += swap(cs_ref[...]).astype(F32)
    for g_ref, base in ((top_ref, 0), (low_ref, 16)):

        @pl.loop(0, 8)
        def _(k):
            rows = pl.ds(base + 2 * k, 2)
            pre = pre_ref[rows]
            s = jax.nn.sigmoid(pre)
            hid_ref[rows] = (pre * s).astype(BF)
            g_ref[pl.ds(2 * k, 2)] = (hg_ref[rows] * s * (1.0 + pre * (1.0 - s))).astype(BF)

    for g_ref, c_ref, base in ((top_ref, ct_ref, 0), (low_ref, cl_ref, 16)):
        gi_ref[base : base + 16] = g_ref[:, inner, :]
        edge = g_ref[:, outer, :]
        go_ref[base : base + 16] = edge
        c_ref[...] = edge


def proj_kernel(hid_ref, cot_ref, proj_ref, top_ref, low_ref, out_ref, pw_ref, bias_ref):
    hidden = px(hid_ref, 0, 32, 0, 48)
    cot = px(cot_ref, 0, 32, 0, 48)
    out_ref[...] = dot(hidden, proj_ref[...]).astype(BF).reshape(32, 48, 256)
    pw_ref[...] = dot(hidden, cot, TN)
    total = px(top_ref, 0, 16, 0, 48).astype(F32) + px(low_ref, 0, 16, 0, 48).astype(F32)
    bias_ref[...] = jnp.sum(total, axis=0, keepdims=True)


def edge_kernel(core_ref, top_ref, low_ref, edge_ref):
    cols = pl.ds(pl.multiple_of(32 - 32 * core_ref[0], 16), 16)
    edge_ref[0:16] = top_ref[:, cols, :]
    edge_ref[16:32] = low_ref[:, cols, :]


def wgrad_kernel(
    core_ref, ft_ref, gt_ref, gl_ref, ht_ref, hl_ref, hi_ref, ho_ref, ct_ref, cl_ref, edge_ref, em_ref, eo_ref,
    g_ref, mine_ref, other_ref,
):
    core = core_ref[0]
    inner = pl.ds(pl.multiple_of(64 - 64 * core, 16), 16)
    outer = pl.ds(pl.multiple_of(64 * core, 16), 16)
    g_ref[0:16, 16:64, :] = ht_ref[...]
    g_ref[16:32, 16:64, :] = gt_ref[...]
    g_ref[32:48, 16:64, :] = gl_ref[...]
    g_ref[48:64, 16:64, :] = hl_ref[...]
    g_ref[0:16, inner, :] = swap(edge_ref[0:16])
    g_ref[16:48, inner, :] = swap(hi_ref[...])
    g_ref[48:64, inner, :] = swap(edge_ref[16:32])
    g_ref[0:16, outer, :] = swap(ct_ref[...])
    g_ref[16:48, outer, :] = swap(ho_ref[...])
    g_ref[48:64, outer, :] = swap(cl_ref[...])
    wgrad_part(ft_ref, g_ref, em_ref, eo_ref, mine_ref, other_ref, 0)


def wgrad_part(ft_ref, g_ref, em_ref, eo_ref, mine_ref, other_ref, chip0):
    mine_ref[:, 144:152, :] = em_ref[chip0 : chip0 + 32]
    other_ref[:, 144:152, :] = eo_ref[chip0 : chip0 + 32]
    begin, end = 144 * chip0, 144 * chip0 + 4608
    for t in range(9):
        first, last = max(begin, 1024 * t), min(end, 1024 * t + 1024)
        if first >= last:
            continue
        row, col = (2 - t // 3) * D, (2 - t % 3) * D
        blocks = [
            px(g_ref, row + 16 * i, row + 16 * i + 16, col + 16 * j, col + 16 * j + 16)
            for i in range(2)
            for j in range(3)
        ]
        res = dot(ft_ref[first - 1024 * t : last - 1024 * t], jnp.concatenate(blocks, axis=0)).astype(BF)
        at = first
        while at < last:
            chip, r = divmod(at, 144)
            size = min(144 - r, last - at)
            mine_ref[chip - chip0, r : r + size, :] = res[at - first : at - first + size, :128]
            other_ref[chip - chip0, r : r + size, :] = res[at - first : at - first + size, 128:]
            at += size


def wgrad_rest_kernel(ft_ref, g_ref, em_ref, eo_ref, mine_ref, other_ref):
    wgrad_part(ft_ref, g_ref, em_ref, eo_ref, mine_ref, other_ref, 32)


def add_kernel(m_ref, r_ref, out_ref):
    @pl.loop(0, 16)
    def _(k):
        pair = pl.ds(2 * k, 2)
        out_ref[pair] = (m_ref[pair].astype(F32) + r_ref[pair].astype(F32)).astype(BF)


def add_rest_kernel(first_ref, m_ref, r_ref, out_ref):
    @pl.loop(0, 16)
    def _(k):
        pair = pl.ds(2 * k, 2)
        out_ref[pair] = first_ref[pair]
        out_ref[pl.ds(32 + 2 * k, 2)] = (m_ref[pair].astype(F32) + r_ref[pair].astype(F32)).astype(BF)


def fgrad_kernel(g_ref, mine_ref, other_ref, out_ref):
    @pl.loop(0, 4)
    def _(k):
        acc = None
        for t in range(9):
            row, col = (2 - t // 3) * D, (2 - t % 3) * D
            win = g_ref[pl.ds(row + 8 * k, 8), col : col + 48, :].reshape(384, 256)
            term = dot(win, tap(mine_ref, other_ref, t // 3, t % 3), NT)
            acc = term if acc is None else acc + term
        out_ref[pl.ds(8 * k, 8)] = acc.astype(BF).reshape(8, 48, 1024)


def body(features, conv_weight, conv_bias, proj_weight, cotangent):
    core = lax.axis_index("core")
    is0 = core == 0
    core_s = core.astype(jnp.int32).reshape(1)
    smem = pl.BlockSpec(memory_space=pltpu.SMEM)

    def send(x, dr, dc):
        perm = []
        for i in range(128):
            r, c = i // 8 + dr, i % 8 + dc[i % 2]
            if 0 <= r < 16 and 0 <= c < 8:
                perm.append((i, r * 8 + c))
        return lax.ppermute(x, ALL, perm)

    def array(shape, dtype=BF):
        return jax.ShapeDtypeStruct(shape, dtype)

    def call(kernel, name, outs, args, flops, size, scratch=()):
        specs = [smem if a is core_s else vmem() for a in args]
        return pl.pallas_call(
            kernel,
            out_shape=tuple(outs),
            in_specs=specs,
            out_specs=(vmem(),) * len(outs),
            scratch_shapes=list(scratch),
            compiler_params=params(),
            cost_estimate=cost(int(flops), int(size)),
            name=name,
        )(*args)

    SAME, INNER, OUTER = (0, 0), (1, -1), (-1, 1)

    low, high = conv_weight[:, :128], conv_weight[:, 128:]
    own_proj = jnp.concatenate([proj_weight[:, :128], proj_weight[:, 128:]], axis=0)
    got = send(jnp.concatenate([jnp.where(is0, high, low), own_proj], axis=0), 0, INNER)
    keep = jnp.concatenate([jnp.where(is0, low, high), own_proj], axis=0)
    even, odd = jnp.where(is0, keep, got), jnp.where(is0, got, keep)
    chunk = jnp.concatenate([even[:72], odd[:72], even[72:74], odd[72:74], even[74:76], odd[74:76]], axis=0)
    mine = lax.all_to_all(jnp.broadcast_to(chunk[None], (64, 152, 128)), CHIPS, 0, 0)
    (ft,) = call(flip_kernel, "flip", [array((1024, 1536))], [features], 1e6, 6e6)
    mine, ft = lax.optimization_barrier((mine, ft))
    other = send(mine, 0, INNER)
    (proj,) = call(rows_kernel, "rows", [array((256, 256))], [core_s, mine], 1e6, 1e6, [pltpu.VMEM((256, 256), F32)])
    other, proj = lax.optimization_barrier((other, proj))
    bias = jnp.where(is0, conv_bias, jnp.concatenate([conv_bias[128:], conv_bias[:128]])).reshape(1, 256)

    tile, strip, small, side = (32, 48, 256), (16, 48, 256), (16, 16, 256), (32, 16, 256)
    n, s, inner, outer, cn, cs = call(
        halo_kernel,
        "halo",
        [array(strip), array(strip), array((64, 16, 256)), array(side), array(small), array(small)],
        [core_s, features, mine, other],
        3.5e9,
        9e6,
        [pltpu.VMEM((2, 64, 16, 256), BF), pltpu.VMEM((16, 80, 256), F32)],
    )
    inner = send(inner, 0, INNER)
    n, s = call(merge_kernel, "merge", [array(strip), array(strip)], [core_s, n, s, inner], 1e6, 2e6)
    from_s = send(n, -1, SAME)
    from_n = send(s, 1, SAME)
    outer = send(outer, 0, OUTER)
    corner_s = send(cn, -1, OUTER)
    corner_n = send(cs, 1, OUTER)

    own, hg = call(
        own_kernel,
        "own",
        [array(tile, F32), array(tile, F32)],
        [features, mine, other, cotangent, proj, bias],
        4e9,
        12e6,
    )
    hidden, g_top, g_low, gi, go, ct, cl = call(
        point_kernel,
        "point",
        [array(tile), array(strip), array(strip), array(side), array(side), array(small), array(small)],
        [core_s, own, hg, from_n, from_s, inner, outer, corner_n, corner_s],
        1e8,
        6e6,
        [pltpu.VMEM(tile, F32)],
    )

    h_top = send(g_low, 1, SAME)
    h_low = send(g_top, -1, SAME)
    h_outer = send(go, 0, OUTER)
    c_top = send(cl, 1, OUTER)
    c_low = send(ct, -1, OUTER)
    h_inner = send(gi, 0, INNER)

    projected, pw, bias_term = call(
        proj_kernel,
        "proj",
        [array(tile), array((256, 256), F32), array((1, 256), F32)],
        [hidden, cotangent, proj, g_top, g_low],
        4e8,
        4e6,
    )
    pw = jnp.where(is0, pw, jnp.concatenate([pw[128:], pw[:128]], axis=0)).astype(BF)
    bias_term = jnp.where(is0, bias_term, jnp.concatenate([bias_term[:, 128:], bias_term[:, :128]], axis=1))
    bias_rows = jnp.pad(bias_term.astype(BF).reshape(64, 1, 4), ((0, 0), (0, 3), (0, 124)))

    def extra(p):
        return jnp.concatenate([p.reshape(64, 4, 128), bias_rows], axis=1)

    e_mine = extra(jnp.where(is0, pw[:, :128], pw[:, 128:]))
    e_other = extra(jnp.where(is0, pw[:, 128:], pw[:, :128]))

    h_top, h_low, c_top, c_low, h_outer = lax.optimization_barrier((h_top, h_low, c_top, c_low, h_outer))
    (edge,) = call(edge_kernel, "edge", [array(side)], [core_s, h_top, h_low], 1e6, 1e6)
    edge = send(edge, 0, INNER)
    half = array((32, 152, 128))
    g, m1, o1 = call(
        wgrad_kernel,
        "wgrad",
        [array((64, 80, 256)), half, half],
        [core_s, ft, g_top, g_low, h_top, h_low, h_inner, h_outer, c_top, c_low, edge, e_mine, e_other],
        3.6e9,
        8e6,
    )
    r1 = send(o1, 0, INNER)
    m2, o2 = call(wgrad_rest_kernel, "wgrad2", [half, half], [ft, g, e_mine, e_other], 3.6e9, 8e6)
    r2 = send(o2, 0, INNER)
    (t1,) = call(add_kernel, "add", [half], [m1, r1], 1e6, 4e6)
    (total,) = call(add_rest_kernel, "add2", [array((64, 152, 128))], [t1, m2, r2], 1e6, 7e6)
    pieces = lax.all_to_all(total, CHIPS, 0, 0)

    (features_grad,) = call(fgrad_kernel, "fgrad", [array((32, 48, 1024))], [g, mine, other], 7.2e9, 12e6)

    sums = jnp.sum(pieces.astype(F32), axis=0)
    lo, hi = jnp.concatenate([sums[:72], sums[144:146]], 0), jnp.concatenate([sums[72:144], sums[146:148]], 0)
    keep = jnp.where(is0, lo, hi)
    got = send(jnp.where(is0, hi, lo), 0, INNER)
    both = jnp.concatenate([jnp.where(is0, keep, got), jnp.where(is0, got, keep)], axis=1)
    bias_grad = jnp.where(is0, sums[148, 0:2], sums[148, 2:4])
    return projected, features_grad, both[:72], both[72:74], bias_grad


def solution(mesh):
    fine = Mesh(mesh.devices.reshape(4, 4, 4, 2), ALL)
    tile = P(("y", "x"), ("z", "core"), None)
    rows = P(ALL, None)
    return jax.shard_map(
        body,
        mesh=fine,
        in_specs=(tile, rows, P(), rows, tile),
        out_specs=(tile, tile, rows, rows, P(ALL)),
        check_vma=False,
    )
```

```python
import jax
import jax.numpy as jnp
import numpy as np
from jax import lax
from jax.experimental import pallas as pl
from jax.experimental.pallas import tpu as pltpu
from jax.sharding import Mesh, PartitionSpec as P

D = 16
CHIPS = ("y", "x", "z")
ALL = ("y", "x", "z", "core")
BF = jnp.bfloat16
F32 = jnp.float32
VMEM_LIMIT = 18 * 1024 * 1024

NN = (((1,), (0,)), ((), ()))
NT = (((1,), (1,)), ((), ()))
TN = (((0,), (0,)), ((), ()))


def dot(a, b, dims=NN):
    return lax.dot_general(a, b, dims, preferred_element_type=F32)


def vmem():
    return pl.BlockSpec(memory_space=pltpu.VMEM)


def params():
    return pltpu.CompilerParams(vmem_limit_bytes=VMEM_LIMIT)


def cost(flops, size):
    return pl.CostEstimate(flops=flops, bytes_accessed=size, transcendentals=0)


def swap(x):
    return jnp.concatenate([x[..., 128:], x[..., :128]], axis=-1)


def tap(mine_ref, other_ref, a, b):
    row = (3 * a + b) * 1024
    first, last = row // 144, -(-(row + 1024) // 144)
    skip = row - 144 * first

    def half(ref):
        return ref[first:last, 0:144, :].reshape((last - first) * 144, 128)[skip : skip + 1024]

    return jnp.concatenate([half(mine_ref), half(other_ref)], axis=1)


def px(ref, r0, r1, c0, c1):
    return ref[r0:r1, c0:c1, :].reshape((r1 - r0) * (c1 - c0), ref.shape[2])


def give_kernel(core_ref, conv_ref, proj_ref, keep_ref, give_ref, acc):
    first = core_ref[0] == 0
    low, high = conv_ref[:, :128].astype(F32), conv_ref[:, 128:].astype(F32)
    proj = proj_ref[...].astype(F32)
    acc[...] = jnp.zeros_like(acc)
    acc[72:74] = proj[:, :128]
    acc[74:76] = proj[:, 128:]
    acc[0:72] = jnp.where(first, low, high)
    keep_ref[...] = acc[...].astype(BF)
    acc[0:72] = jnp.where(first, high, low)
    give_ref[...] = acc[...].astype(BF)


def spread_kernel(core_ref, keep_ref, got_ref, out_ref, acc):
    first = core_ref[0] == 0
    keep, got = keep_ref[...].astype(F32), got_ref[...].astype(F32)
    even, odd = jnp.where(first, keep, got), jnp.where(first, got, keep)
    acc[0:72] = even[0:72]
    acc[72:144] = odd[0:72]
    acc[144:146] = even[72:74]
    acc[146:148] = odd[72:74]
    acc[148:150] = even[74:76]
    acc[150:152] = odd[74:76]
    chunk = acc[...].astype(BF)

    @pl.loop(0, 64)
    def _(k):
        out_ref[k] = chunk


def flip_kernel(f_ref, ft_ref):
    for k in range(6):
        i, j = divmod(k, 3)
        block = px(f_ref, 16 * i, 16 * i + 16, 16 * j, 16 * j + 16)
        ft_ref[:, 256 * k : 256 * k + 256] = block.T


def rows_kernel(core_ref, mine_ref, proj_ref, acc):
    for k in range(64):
        x = mine_ref[k, 144:152, :].astype(F32)
        acc[4 * k : 4 * k + 4, :128] = x[0:4]
        acc[4 * k : 4 * k + 4, 128:] = x[4:8]
    start = pl.multiple_of(128 * core_ref[0], 128)
    proj_ref[0:128] = acc[pl.ds(start, 128), :].astype(BF)
    proj_ref[128:256] = acc[pl.ds(128 - start, 128), :].astype(BF)


def halo_kernel(core_ref, f_ref, mine_ref, other_ref, n_ref, s_ref, inner_ref, outer_ref, cn_ref, cs_ref, sides, acc):
    core = core_ref[0]
    for out, a, r0, block in ((n_ref, 2, 0, 0), (s_ref, 0, 16, 3)):
        acc[...] = jnp.zeros_like(acc)
        for b in range(3):
            c = (2 - b) * D
            acc[:, c : c + 48, :] += dot(px(f_ref, r0, r0 + 16, 0, 48), tap(mine_ref, other_ref, a, b)).reshape(
                16, 48, 256
            )
        sides[0, 16 * block : 16 * block + 16] = acc[:, 0:16, :].astype(BF)
        out[...] = acc[:, 16:64, :].astype(BF)
        sides[1, 16 * block : 16 * block + 16] = acc[:, 64:80, :].astype(BF)
    for side, b, c0 in ((0, 2, 0), (1, 0, 32)):
        mid = dot(px(f_ref, 0, 32, c0, c0 + 16), tap(mine_ref, other_ref, 1, b))
        top = mid[:256] + dot(px(f_ref, 16, 32, c0, c0 + 16), tap(mine_ref, other_ref, 2, b))
        low = mid[256:] + dot(px(f_ref, 0, 16, c0, c0 + 16), tap(mine_ref, other_ref, 0, b))
        sides[side, 16:32] = top.reshape(16, 16, 256).astype(BF)
        sides[side, 32:48] = low.reshape(16, 16, 256).astype(BF)
    inner_ref[...] = sides[1 - core]
    outer_ref[...] = sides[core, 16:48]
    cn_ref[...] = sides[core, 0:16]
    cs_ref[...] = sides[core, 48:64]


def merge_kernel(core_ref, n_ref, s_ref, inner_ref, no_ref, so_ref):
    cols = pl.ds(pl.multiple_of(32 - 32 * core_ref[0], 16), 16)
    for src, dst, r in ((n_ref, no_ref, 0), (s_ref, so_ref, 48)):
        dst[...] = src[...]
        dst[:, cols, :] = (src[:, cols, :].astype(F32) + swap(inner_ref[r : r + 16]).astype(F32)).astype(BF)


def own_kernel(core_ref, f_ref, mine_ref, other_ref, cot_ref, proj_ref, bias_ref, pre_ref, hg_ref):
    first = dot(px(f_ref, 0, 32, 0, 48), tap(mine_ref, other_ref, 1, 1))
    bias = bias_ref[...]
    bias = jnp.where(core_ref[0] == 0, bias, swap(bias))
    pre_ref[...] = (first + bias).reshape(32, 48, 256)
    for a, rows in ((0, ((0, 16), (16, 32))), (1, ((0, 32), (0, 32))), (2, ((16, 32), (0, 16)))):
        for b, cols in ((0, ((0, 32), (16, 48))), (1, ((0, 48), (0, 48))), (2, ((16, 48), (0, 32)))):
            if a == 1 and b == 1:
                continue
            (fr, pr), (fc, pc) = rows, cols
            pre_ref[pr[0] : pr[1], pc[0] : pc[1], :] += dot(
                px(f_ref, *fr, *fc), tap(mine_ref, other_ref, a, b)
            ).reshape(pr[1] - pr[0], pc[1] - pc[0], 256)
    hg_ref[...] = dot(px(cot_ref, 0, 32, 0, 48), proj_ref[...], NT).reshape(32, 48, 256)


def point_kernel(
    core_ref, own_ref, hg_ref, n_ref, s_ref, inner_ref, outer_ref, cn_ref, cs_ref,
    hid_ref, top_ref, low_ref, gi_ref, go_ref, ct_ref, cl_ref, pre_ref,
):
    core = core_ref[0]
    inner = pl.ds(pl.multiple_of(32 - 32 * core, 16), 16)
    outer = pl.ds(pl.multiple_of(32 * core, 16), 16)
    pre_ref[0:16] = own_ref[0:16] + n_ref[...].astype(F32)
    pre_ref[16:32] = own_ref[16:32] + s_ref[...].astype(F32)
    pre_ref[:, inner, :] += swap(inner_ref[16:48]).astype(F32)
    pre_ref[:, outer, :] += swap(outer_ref[...]).astype(F32)
    pre_ref[0:16, outer, :] += swap(cn_ref[...]).astype(F32)
    pre_ref[16:32, outer, :] += swap(cs_ref[...]).astype(F32)
    for g_ref, base in ((top_ref, 0), (low_ref, 16)):

        @pl.loop(0, 8)
        def _(k):
            rows = pl.ds(base + 2 * k, 2)
            pre = pre_ref[rows]
            s = jax.nn.sigmoid(pre)
            hid_ref[rows] = (pre * s).astype(BF)
            g_ref[pl.ds(2 * k, 2)] = (hg_ref[rows] * s * (1.0 + pre * (1.0 - s))).astype(BF)

    for g_ref, c_ref, base in ((top_ref, ct_ref, 0), (low_ref, cl_ref, 16)):
        gi_ref[base : base + 16] = g_ref[:, inner, :]
        edge = g_ref[:, outer, :]
        go_ref[base : base + 16] = edge
        c_ref[...] = edge


def proj_kernel(core_ref, hid_ref, cot_ref, proj_ref, top_ref, low_ref, out_ref, em_ref, eo_ref, pw, ext):
    first = core_ref[0] == 0
    start = pl.multiple_of(128 * core_ref[0], 128)
    hidden = px(hid_ref, 0, 32, 0, 48)
    cot = px(cot_ref, 0, 32, 0, 48)
    out_ref[...] = dot(hidden, proj_ref[...]).astype(BF).reshape(32, 48, 256)
    term = dot(hidden, cot, TN)
    term = jnp.where(first, term, swap(term))
    pw[pl.ds(start, 128), :] = term[0:128]
    pw[pl.ds(128 - start, 128), :] = term[128:256]
    total = px(top_ref, 0, 16, 0, 48).astype(F32) + px(low_ref, 0, 16, 0, 48).astype(F32)
    bias = jnp.sum(total, axis=0, keepdims=True)
    bias = jnp.where(first, bias, swap(bias))
    for e_ref, c in ((em_ref, 0), (eo_ref, 128)):
        for k in range(64):
            ext[k, 0:4] = pw[4 * k : 4 * k + 4, c : c + 128]
            ext[k, 4:8] = jnp.broadcast_to(bias[:, 128 * (k // 32) : 128 * (k // 32) + 128], (4, 128))
        e_ref[...] = ext[...].astype(BF)


def edge_kernel(core_ref, top_ref, low_ref, edge_ref):
    cols = pl.ds(pl.multiple_of(32 - 32 * core_ref[0], 16), 16)
    edge_ref[0:16] = top_ref[:, cols, :]
    edge_ref[16:32] = low_ref[:, cols, :]


def wgrad_kernel(
    core_ref, ft_ref, gt_ref, gl_ref, ht_ref, hl_ref, hi_ref, ho_ref, ct_ref, cl_ref, edge_ref, em_ref, eo_ref,
    g_ref, mine_ref, other_ref,
):
    core = core_ref[0]
    inner = pl.ds(pl.multiple_of(64 - 64 * core, 16), 16)
    outer = pl.ds(pl.multiple_of(64 * core, 16), 16)
    g_ref[0:16, 16:64, :] = ht_ref[...]
    g_ref[16:32, 16:64, :] = gt_ref[...]
    g_ref[32:48, 16:64, :] = gl_ref[...]
    g_ref[48:64, 16:64, :] = hl_ref[...]
    g_ref[0:16, inner, :] = swap(edge_ref[0:16])
    g_ref[16:48, inner, :] = swap(hi_ref[...])
    g_ref[48:64, inner, :] = swap(edge_ref[16:32])
    g_ref[0:16, outer, :] = swap(ct_ref[...])
    g_ref[16:48, outer, :] = swap(ho_ref[...])
    g_ref[48:64, outer, :] = swap(cl_ref[...])
    wgrad_part(ft_ref, g_ref, em_ref, eo_ref, mine_ref, other_ref, 0)


def wgrad_part(ft_ref, g_ref, em_ref, eo_ref, mine_ref, other_ref, chip0):
    mine_ref[:, 144:152, :] = em_ref[chip0 : chip0 + 32]
    other_ref[:, 144:152, :] = eo_ref[chip0 : chip0 + 32]
    begin, end = 144 * chip0, 144 * chip0 + 4608
    for t in range(9):
        first, last = max(begin, 1024 * t), min(end, 1024 * t + 1024)
        if first >= last:
            continue
        row, col = (2 - t // 3) * D, (2 - t % 3) * D
        blocks = [
            px(g_ref, row + 16 * i, row + 16 * i + 16, col + 16 * j, col + 16 * j + 16)
            for i in range(2)
            for j in range(3)
        ]
        res = dot(ft_ref[first - 1024 * t : last - 1024 * t], jnp.concatenate(blocks, axis=0)).astype(BF)
        at = first
        while at < last:
            chip, r = divmod(at, 144)
            size = min(144 - r, last - at)
            mine_ref[chip - chip0, r : r + size, :] = res[at - first : at - first + size, :128]
            other_ref[chip - chip0, r : r + size, :] = res[at - first : at - first + size, 128:]
            at += size


def wgrad_rest_kernel(ft_ref, g_ref, em_ref, eo_ref, mine_ref, other_ref):
    wgrad_part(ft_ref, g_ref, em_ref, eo_ref, mine_ref, other_ref, 32)


def add_kernel(m_ref, r_ref, out_ref):
    @pl.loop(0, 16)
    def _(k):
        pair = pl.ds(2 * k, 2)
        out_ref[pair] = (m_ref[pair].astype(F32) + r_ref[pair].astype(F32)).astype(BF)


def add_rest_kernel(first_ref, m_ref, r_ref, out_ref):
    @pl.loop(0, 16)
    def _(k):
        pair = pl.ds(2 * k, 2)
        out_ref[pair] = first_ref[pair]
        out_ref[pl.ds(32 + 2 * k, 2)] = (m_ref[pair].astype(F32) + r_ref[pair].astype(F32)).astype(BF)


def sum_kernel(core_ref, in_ref, keep_ref, give_ref, bias_ref, acc):
    acc[...] = in_ref[0].astype(F32)

    @pl.loop(1, 64)
    def _(k):
        acc[...] += in_ref[k].astype(F32)

    bias_ref[...] = acc[148:149]
    for out, c in ((keep_ref, core_ref[0]), (give_ref, 1 - core_ref[0])):
        out[0:72] = acc[pl.ds(pl.multiple_of(72 * c, 8), 72)]
        out[72:80] = jnp.where(c == 0, acc[144:152], pltpu.roll(acc[144:152], 6, 0))


def join_kernel(core_ref, keep_ref, got_ref, conv_ref, proj_ref):
    first = core_ref[0] == 0
    keep, got = keep_ref[...], got_ref[...]
    both = jnp.concatenate([jnp.where(first, keep, got), jnp.where(first, got, keep)], axis=1)
    conv_ref[...] = both[0:72]
    proj_ref[...] = both[72:74]


def fgrad_kernel(g_ref, mine_ref, other_ref, out_ref):
    @pl.loop(0, 4)
    def _(k):
        acc = None
        for t in range(9):
            row, col = (2 - t // 3) * D, (2 - t % 3) * D
            win = g_ref[pl.ds(row + 8 * k, 8), col : col + 48, :].reshape(384, 256)
            term = dot(win, tap(mine_ref, other_ref, t // 3, t % 3), NT)
            acc = term if acc is None else acc + term
        out_ref[pl.ds(8 * k, 8)] = acc.astype(BF).reshape(8, 48, 1024)


def body(features, conv_weight, conv_bias, proj_weight, cotangent):
    core = lax.axis_index("core")
    core_s = core.astype(jnp.int32).reshape(1)
    smem = pl.BlockSpec(memory_space=pltpu.SMEM)

    def send(x, dr, dc):
        perm = []
        for i in range(128):
            r, c = i // 8 + dr, i % 8 + dc[i % 2]
            if 0 <= r < 16 and 0 <= c < 8:
                perm.append((i, r * 8 + c))
        return lax.ppermute(x, ALL, perm)

    def array(shape, dtype=BF):
        return jax.ShapeDtypeStruct(shape, dtype)

    def call(kernel, name, outs, args, flops, size, scratch=()):
        specs = [smem if a is core_s else vmem() for a in args]
        return pl.pallas_call(
            kernel,
            out_shape=tuple(outs),
            in_specs=specs,
            out_specs=(vmem(),) * len(outs),
            scratch_shapes=list(scratch),
            compiler_params=params(),
            cost_estimate=cost(int(flops), int(size)),
            name=name,
        )(*args)

    SAME, INNER, OUTER = (0, 0), (1, -1), (-1, 1)

    pack = array((80, 128))
    keep, give = call(
        give_kernel, "give", [pack, pack], [core_s, conv_weight, proj_weight], 1e5, 1e5, [pltpu.VMEM((80, 128), F32)]
    )
    got = send(give, 0, INNER)
    (spread,) = call(
        spread_kernel,
        "spread",
        [array((64, 152, 128))],
        [core_s, keep, got],
        1e5,
        3e6,
        [pltpu.VMEM((152, 128), F32)],
    )
    mine = lax.all_to_all(spread, CHIPS, 0, 0)
    (ft,) = call(flip_kernel, "flip", [array((1024, 1536))], [features], 1e6, 6e6)
    mine, ft = lax.optimization_barrier((mine, ft))
    other = send(mine, 0, INNER)
    (proj,) = call(rows_kernel, "rows", [array((256, 256))], [core_s, mine], 1e6, 1e6, [pltpu.VMEM((256, 256), F32)])
    other, proj = lax.optimization_barrier((other, proj))
    tile, strip, small, side = (32, 48, 256), (16, 48, 256), (16, 16, 256), (32, 16, 256)
    n, s, inner, outer, cn, cs = call(
        halo_kernel,
        "halo",
        [array(strip), array(strip), array((64, 16, 256)), array(side), array(small), array(small)],
        [core_s, features, mine, other],
        3.5e9,
        9e6,
        [pltpu.VMEM((2, 64, 16, 256), BF), pltpu.VMEM((16, 80, 256), F32)],
    )
    inner = send(inner, 0, INNER)
    n, s = call(merge_kernel, "merge", [array(strip), array(strip)], [core_s, n, s, inner], 1e6, 2e6)
    from_s = send(n, -1, SAME)
    from_n = send(s, 1, SAME)
    outer = send(outer, 0, OUTER)
    corner_s = send(cn, -1, OUTER)
    corner_n = send(cs, 1, OUTER)

    own, hg = call(
        own_kernel,
        "own",
        [array(tile, F32), array(tile, F32)],
        [core_s, features, mine, other, cotangent, proj, conv_bias.reshape(1, 256)],
        4e9,
        12e6,
    )
    hidden, g_top, g_low, gi, go, ct, cl = call(
        point_kernel,
        "point",
        [array(tile), array(strip), array(strip), array(side), array(side), array(small), array(small)],
        [core_s, own, hg, from_n, from_s, inner, outer, corner_n, corner_s],
        1e8,
        6e6,
        [pltpu.VMEM(tile, F32)],
    )

    h_top = send(g_low, 1, SAME)
    h_low = send(g_top, -1, SAME)
    h_outer = send(go, 0, OUTER)
    c_top = send(cl, 1, OUTER)
    c_low = send(ct, -1, OUTER)
    h_inner = send(gi, 0, INNER)

    ends = array((64, 8, 128))
    projected, e_mine, e_other = call(
        proj_kernel,
        "proj",
        [array(tile), ends, ends],
        [core_s, hidden, cotangent, proj, g_top, g_low],
        4e9,
        4e6,
        [pltpu.VMEM((256, 256), F32), pltpu.VMEM((64, 8, 128), F32)],
    )
    h_top, h_low, c_top, c_low, h_outer = lax.optimization_barrier((h_top, h_low, c_top, c_low, h_outer))
    (edge,) = call(edge_kernel, "edge", [array(side)], [core_s, h_top, h_low], 1e6, 1e6)
    edge = send(edge, 0, INNER)
    half = array((32, 152, 128))
    g, m1, o1 = call(
        wgrad_kernel,
        "wgrad",
        [array((64, 80, 256)), half, half],
        [core_s, ft, g_top, g_low, h_top, h_low, h_inner, h_outer, c_top, c_low, edge, e_mine, e_other],
        3.6e9,
        8e6,
    )
    r1 = send(o1, 0, INNER)
    m2, o2 = call(wgrad_rest_kernel, "wgrad2", [half, half], [ft, g, e_mine, e_other], 3.6e9, 8e6)
    r2 = send(o2, 0, INNER)
    (t1,) = call(add_kernel, "add", [half], [m1, r1], 1e6, 4e6)
    (total,) = call(add_rest_kernel, "add2", [array((64, 152, 128))], [t1, m2, r2], 1e6, 7e6)
    pieces = lax.all_to_all(total, CHIPS, 0, 0)

    (features_grad,) = call(fgrad_kernel, "fgrad", [array((32, 48, 1024))], [g, mine, other], 7.2e9, 12e6)

    pack = array((80, 128), F32)
    keep, give, bias_row = call(
        sum_kernel,
        "sum",
        [pack, pack, array((1, 128), F32)],
        [core_s, pieces],
        1e6,
        3e6,
        [pltpu.VMEM((152, 128), F32)],
    )
    got = send(give, 0, INNER)
    conv_grad, proj_grad = call(
        join_kernel, "join", [array((72, 256), F32), array((2, 256), F32)], [core_s, keep, got], 1e5, 1e5
    )
    here = 2 * lax.axis_index(ALL) % 128
    bias_grad = lax.dynamic_slice(bias_row.reshape(128), (here,), (2,))
    return projected, features_grad, conv_grad, proj_grad, bias_grad


def solution(mesh):
    fine = Mesh(mesh.devices.reshape(4, 4, 4, 2), ALL)
    tile = P(("y", "x"), ("z", "core"), None)
    rows = P(ALL, None)
    return jax.shard_map(
        body,
        mesh=fine,
        in_specs=(tile, rows, P(), rows, tile),
        out_specs=(tile, tile, rows, rows, P(ALL)),
        check_vma=False,
    )
```

```python
import functools

import jax
import jax.numpy as jnp
import numpy as np
from jax import lax
from jax.experimental import pallas as pl
from jax.experimental.pallas import tpu as pltpu
from jax.sharding import Mesh, PartitionSpec as P

D = 16
CHIPS = ("y", "x", "z")
ALL = ("y", "x", "z", "core")
BF = jnp.bfloat16
F32 = jnp.float32
VMEM_LIMIT = 18 * 1024 * 1024

NN = (((1,), (0,)), ((), ()))
NT = (((1,), (1,)), ((), ()))
TN = (((0,), (0,)), ((), ()))


def dot(a, b, dims=NN):
    return lax.dot_general(a, b, dims, preferred_element_type=F32)


def vmem():
    return pl.BlockSpec(memory_space=pltpu.VMEM)


def any_space():
    return pl.BlockSpec(memory_space=pl.ANY)


def params(limit):
    return pltpu.CompilerParams(vmem_limit_bytes=limit)


def cost(flops, size):
    return pl.CostEstimate(flops=flops, bytes_accessed=size, transcendentals=0)


def swap(x):
    return jnp.concatenate([x[..., 128:], x[..., :128]], axis=-1)


def tap(mine_ref, other_ref, a, b):
    row = (3 * a + b) * 1024
    first, last = row // 144, -(-(row + 1024) // 144)
    skip = row - 144 * first

    def half(ref):
        return ref[first:last, 0:144, :].reshape((last - first) * 144, 128)[skip : skip + 1024]

    return jnp.concatenate([half(mine_ref), half(other_ref)], axis=1)


def px(ref, r0, r1, c0, c1):
    return ref[r0:r1, c0:c1, :].reshape((r1 - r0) * (c1 - c0), ref.shape[2])


def give_kernel(core_ref, conv_ref, proj_ref, keep_ref, give_ref, acc):
    first = core_ref[0] == 0
    low, high = conv_ref[:, :128].astype(F32), conv_ref[:, 128:].astype(F32)
    proj = proj_ref[...].astype(F32)
    acc[...] = jnp.zeros_like(acc)
    acc[72:74] = proj[:, :128]
    acc[74:76] = proj[:, 128:]
    acc[0:72] = jnp.where(first, low, high)
    keep_ref[...] = acc[...].astype(BF)
    acc[0:72] = jnp.where(first, high, low)
    give_ref[...] = acc[...].astype(BF)


def spread_kernel(core_ref, keep_ref, got_ref, out_ref, acc, many, sems):
    first = core_ref[0] == 0
    keep, got = keep_ref[...].astype(F32), got_ref[...].astype(F32)
    even, odd = jnp.where(first, keep, got), jnp.where(first, got, keep)
    acc[0:72] = even[0:72]
    acc[72:144] = odd[0:72]
    acc[144:146] = even[72:74]
    acc[146:148] = odd[72:74]
    acc[148:150] = even[74:76]
    acc[150:152] = odd[74:76]
    chunk = acc[...].astype(BF)
    for k in range(8):
        many[k] = chunk
    copies = [pltpu.make_async_copy(many, out_ref.at[pl.ds(8 * k, 8)], sems.at[k]) for k in range(8)]
    for copy in copies:
        copy.start()
    for copy in copies:
        copy.wait()


def flip_kernel(f_ref, ft_ref):
    for k in range(6):
        i, j = divmod(k, 3)
        block = px(f_ref, 16 * i, 16 * i + 16, 16 * j, 16 * j + 16)
        ft_ref[:, 256 * k : 256 * k + 256] = block.T


def rows_kernel(core_ref, mine_ref, proj_ref, acc):
    for k in range(64):
        x = mine_ref[k, 144:152, :].astype(F32)
        acc[4 * k : 4 * k + 4, :128] = x[0:4]
        acc[4 * k : 4 * k + 4, 128:] = x[4:8]
    start = pl.multiple_of(128 * core_ref[0], 128)
    proj_ref[0:128] = acc[pl.ds(start, 128), :].astype(BF)
    proj_ref[128:256] = acc[pl.ds(128 - start, 128), :].astype(BF)


def halo_kernel(core_ref, f_ref, mine_ref, other_ref, n_ref, s_ref, inner_ref, outer_ref, cn_ref, cs_ref, sides, acc):
    core = core_ref[0]
    for out, a, r0, block in ((n_ref, 2, 0, 0), (s_ref, 0, 16, 3)):
        acc[...] = jnp.zeros_like(acc)
        for b in range(3):
            c = (2 - b) * D
            acc[:, c : c + 48, :] += dot(px(f_ref, r0, r0 + 16, 0, 48), tap(mine_ref, other_ref, a, b)).reshape(
                16, 48, 256
            )
        sides[0, 16 * block : 16 * block + 16] = acc[:, 0:16, :].astype(BF)
        out[...] = acc[:, 16:64, :].astype(BF)
        sides[1, 16 * block : 16 * block + 16] = acc[:, 64:80, :].astype(BF)
    for side, b, c0 in ((0, 2, 0), (1, 0, 32)):
        mid = dot(px(f_ref, 0, 32, c0, c0 + 16), tap(mine_ref, other_ref, 1, b))
        top = mid[:256] + dot(px(f_ref, 16, 32, c0, c0 + 16), tap(mine_ref, other_ref, 2, b))
        low = mid[256:] + dot(px(f_ref, 0, 16, c0, c0 + 16), tap(mine_ref, other_ref, 0, b))
        sides[side, 16:32] = top.reshape(16, 16, 256).astype(BF)
        sides[side, 32:48] = low.reshape(16, 16, 256).astype(BF)
    inner_ref[...] = sides[1 - core]
    outer_ref[...] = sides[core, 16:48]
    cn_ref[...] = sides[core, 0:16]
    cs_ref[...] = sides[core, 48:64]


def merge_kernel(core_ref, n_ref, s_ref, inner_ref, no_ref, so_ref):
    cols = pl.ds(pl.multiple_of(32 - 32 * core_ref[0], 16), 16)
    for src, dst, r in ((n_ref, no_ref, 0), (s_ref, so_ref, 48)):
        dst[...] = src[...]
        dst[:, cols, :] = (src[:, cols, :].astype(F32) + swap(inner_ref[r : r + 16]).astype(F32)).astype(BF)


def own_kernel(core_ref, f_ref, mine_ref, other_ref, cot_ref, proj_ref, bias_ref, pre_ref, hg_ref):
    first = dot(px(f_ref, 0, 32, 0, 48), tap(mine_ref, other_ref, 1, 1))
    bias = bias_ref[...]
    bias = jnp.where(core_ref[0] == 0, bias, swap(bias))
    pre_ref[...] = (first + bias).reshape(32, 48, 256)
    for a, rows in ((0, ((0, 16), (16, 32))), (1, ((0, 32), (0, 32))), (2, ((16, 32), (0, 16)))):
        for b, cols in ((0, ((0, 32), (16, 48))), (1, ((0, 48), (0, 48))), (2, ((16, 48), (0, 32)))):
            if a == 1 and b == 1:
                continue
            (fr, pr), (fc, pc) = rows, cols
            pre_ref[pr[0] : pr[1], pc[0] : pc[1], :] += dot(
                px(f_ref, *fr, *fc), tap(mine_ref, other_ref, a, b)
            ).reshape(pr[1] - pr[0], pc[1] - pc[0], 256)
    hg_ref[...] = dot(px(cot_ref, 0, 32, 0, 48), proj_ref[...], NT).reshape(32, 48, 256)


def point_kernel(
    core_ref, own_ref, hg_ref, n_ref, s_ref, inner_ref, outer_ref, cn_ref, cs_ref,
    hid_ref, top_ref, low_ref, gi_ref, go_ref, ct_ref, cl_ref, pre_ref,
):
    core = core_ref[0]
    inner = pl.ds(pl.multiple_of(32 - 32 * core, 16), 16)
    outer = pl.ds(pl.multiple_of(32 * core, 16), 16)
    pre_ref[0:16] = own_ref[0:16] + n_ref[...].astype(F32)
    pre_ref[16:32] = own_ref[16:32] + s_ref[...].astype(F32)
    pre_ref[:, inner, :] += swap(inner_ref[16:48]).astype(F32)
    pre_ref[:, outer, :] += swap(outer_ref[...]).astype(F32)
    pre_ref[0:16, outer, :] += swap(cn_ref[...]).astype(F32)
    pre_ref[16:32, outer, :] += swap(cs_ref[...]).astype(F32)
    for g_ref, base in ((top_ref, 0), (low_ref, 16)):

        @pl.loop(0, 8)
        def _(k):
            rows = pl.ds(base + 2 * k, 2)
            pre = pre_ref[rows]
            s = jax.nn.sigmoid(pre)
            hid_ref[rows] = (pre * s).astype(BF)
            g_ref[pl.ds(2 * k, 2)] = (hg_ref[rows] * s * (1.0 + pre * (1.0 - s))).astype(BF)

    for g_ref, c_ref, base in ((top_ref, ct_ref, 0), (low_ref, cl_ref, 16)):
        gi_ref[base : base + 16] = g_ref[:, inner, :]
        edge = g_ref[:, outer, :]
        go_ref[base : base + 16] = edge
        c_ref[...] = edge


def proj_kernel(core_ref, hid_ref, cot_ref, proj_ref, top_ref, low_ref, out_ref, em_ref, eo_ref, pw, ext):
    first = core_ref[0] == 0
    start = pl.multiple_of(128 * core_ref[0], 128)
    hidden = px(hid_ref, 0, 32, 0, 48)
    cot = px(cot_ref, 0, 32, 0, 48)
    out_ref[...] = dot(hidden, proj_ref[...]).astype(BF).reshape(32, 48, 256)
    term = dot(hidden, cot, TN)
    term = jnp.where(first, term, swap(term))
    pw[pl.ds(start, 128), :] = term[0:128]
    pw[pl.ds(128 - start, 128), :] = term[128:256]
    total = px(top_ref, 0, 16, 0, 48).astype(F32) + px(low_ref, 0, 16, 0, 48).astype(F32)
    bias = jnp.sum(total, axis=0, keepdims=True)
    bias = jnp.where(first, bias, swap(bias))
    for e_ref, c in ((em_ref, 0), (eo_ref, 128)):
        for k in range(64):
            ext[k, 0:4] = pw[4 * k : 4 * k + 4, c : c + 128]
            ext[k, 4:8] = jnp.broadcast_to(bias[:, 128 * (k // 32) : 128 * (k // 32) + 128], (4, 128))
        e_ref[...] = ext[...].astype(BF)


def edge_kernel(core_ref, top_ref, low_ref, edge_ref):
    cols = pl.ds(pl.multiple_of(32 - 32 * core_ref[0], 16), 16)
    edge_ref[0:16] = top_ref[:, cols, :]
    edge_ref[16:32] = low_ref[:, cols, :]


def wgrad_taps(ft_ref, block, a, mine_ref, other_ref):
    for b in range(3):
        blocks = [block(i, 2 - b + j) for i in range(2) for j in range(3)]
        res = dot(ft_ref[...], jnp.concatenate(blocks, axis=0)).astype(BF)
        mine_ref[1024 * b : 1024 * b + 1024] = res[:, :128]
        other_ref[1024 * b : 1024 * b + 1024] = res[:, 128:]


def wgrad_mid_kernel(core_ref, ft_ref, gt_ref, gl_ref, hi_ref, ho_ref, g_ref, mine_ref, other_ref):
    core = core_ref[0]
    inner = pl.ds(pl.multiple_of(64 - 64 * core, 16), 16)
    outer = pl.ds(pl.multiple_of(64 * core, 16), 16)
    g_ref[0:16, 16:64, :] = gt_ref[...]
    g_ref[16:32, 16:64, :] = gl_ref[...]
    g_ref[:, inner, :] = swap(hi_ref[...])
    g_ref[:, outer, :] = swap(ho_ref[...])
    wgrad_taps(
        ft_ref, lambda i, j: px(g_ref, 16 * i, 16 * i + 16, 16 * j, 16 * j + 16), 1, mine_ref, other_ref
    )


def wgrad_row_kernel(a, core_ref, ft_ref, g_ref, h_ref, c_ref, edge_ref, e_ref, row_ref, mine_ref, other_ref):
    core = core_ref[0]
    row_ref[:, 16:64, :] = h_ref[...]
    row_ref[:, pl.ds(pl.multiple_of(64 - 64 * core, 16), 16), :] = swap(edge_ref[8 * (2 - a) : 8 * (2 - a) + 16])
    row_ref[:, pl.ds(pl.multiple_of(64 * core, 16), 16), :] = swap(c_ref[...])

    def block(i, j):
        if a == 0:
            return px(g_ref, 16, 32, 16 * j, 16 * j + 16) if i == 0 else px(row_ref, 0, 16, 16 * j, 16 * j + 16)
        return px(g_ref, 0, 16, 16 * j, 16 * j + 16) if i == 1 else px(row_ref, 0, 16, 16 * j, 16 * j + 16)

    wgrad_taps(ft_ref, block, a, mine_ref, other_ref)
    if a == 0:
        other_ref[3072:3584] = e_ref[...].reshape(512, 128)


def add_kernel(m_ref, r_ref, out_ref):
    @pl.loop(0, 12)
    def _(k):
        rows = pl.ds(pl.multiple_of(256 * k, 256), 256)
        out_ref[rows] = (m_ref[rows].astype(F32) + r_ref[rows].astype(F32)).astype(BF)


def gather_kernel(t0_ref, t1_ref, m2_ref, r2_ref, e_ref, r0_ref, _, out_ref, near, sems):
    copies = []
    for k in range(64):
        at = 144 * k
        while at < 144 * (k + 1):
            part, row = divmod(at, 3072)
            size = min(144 * (k + 1) - at, 3072 - row)
            if part < 2:
                value = (t0_ref, t1_ref)[part][row : row + size]
            else:
                value = (m2_ref[row : row + size].astype(F32) + r2_ref[row : row + size].astype(F32)).astype(BF)
            near[k, at - 144 * k : at - 144 * k + size] = value
            at += size
        ends = e_ref[k].astype(F32) + r0_ref[3072 + 8 * k : 3080 + 8 * k].astype(F32)
        near[k, 144:152] = ends.astype(BF)
        if k % 8 == 7:
            part = pl.ds(k - 7, 8)
            copy = pltpu.make_async_copy(near.at[part], out_ref.at[part], sems.at[k // 8])
            copy.start()
            copies.append(copy)
    for copy in copies:
        copy.wait()


def sum_kernel(core_ref, far_ref, keep_ref, give_ref, bias_ref, acc, near, sems):
    copies = [
        pltpu.make_async_copy(far_ref.at[pl.ds(16 * k, 16)], near.at[pl.ds(16 * k, 16)], sems.at[k]) for k in range(4)
    ]
    for copy in copies:
        copy.start()
    total = jnp.zeros((152, 128), F32)
    for k, copy in enumerate(copies):
        copy.wait()
        total = lax.fori_loop(16 * k, 16 * k + 16, lambda n, t: t + near[n].astype(F32), total, unroll=4)
    acc[...] = total
    bias_ref[...] = acc[148:149]
    for out, c in ((keep_ref, core_ref[0]), (give_ref, 1 - core_ref[0])):
        out[0:72] = acc[pl.ds(pl.multiple_of(72 * c, 8), 72)]
        out[72:80] = jnp.where(c == 0, acc[144:152], pltpu.roll(acc[144:152], 6, 0))


def join_kernel(core_ref, keep_ref, got_ref, conv_ref, proj_ref):
    first = core_ref[0] == 0
    keep, got = keep_ref[...], got_ref[...]
    both = jnp.concatenate([jnp.where(first, keep, got), jnp.where(first, got, keep)], axis=1)
    conv_ref[...] = both[0:72]
    proj_ref[...] = both[72:74]


def fgrad_kernel(top_ref, mid_ref, low_ref, mine_ref, other_ref, out_ref):
    for k in range(4):
        acc = None
        for a in range(3):
            row = 8 * k + (2 - a) * 16
            ref, row = ((top_ref, row), (mid_ref, row - 16), (mid_ref, row - 16), (low_ref, row - 48))[row // 16]
            for b in range(3):
                win = px(ref, row, row + 8, (2 - b) * D, (2 - b) * D + 48)
                term = dot(win, tap(mine_ref, other_ref, a, b), NT)
                acc = term if acc is None else acc + term
        out_ref[8 * k : 8 * k + 8] = acc.astype(BF).reshape(8, 48, 1024)


def body(features, conv_weight, conv_bias, proj_weight, cotangent):
    core = lax.axis_index("core")
    core_s = core.astype(jnp.int32).reshape(1)
    smem = pl.BlockSpec(memory_space=pltpu.SMEM)

    def send(x, dr, dc):
        perm = []
        for i in range(128):
            r, c = i // 8 + dr, i % 8 + dc[i % 2]
            if 0 <= r < 16 and 0 <= c < 8:
                perm.append((i, r * 8 + c))
        return lax.ppermute(x, ALL, perm)

    def array(shape, dtype=BF):
        return jax.ShapeDtypeStruct(shape, dtype)

    def call(kernel, name, outs, args, flops, size, scratch=(), far=(), limit=VMEM_LIMIT, reuse=None):
        specs = [smem if a is core_s else any_space() if any(a is f for f in far) else vmem() for a in args]
        return pl.pallas_call(
            kernel,
            out_shape=tuple(outs),
            in_specs=specs,
            out_specs=((vmem() if limit == VMEM_LIMIT and reuse is None else any_space()),) * len(outs),
            scratch_shapes=list(scratch),
            input_output_aliases={} if reuse is None else {reuse: 0},
            compiler_params=params(limit),
            cost_estimate=cost(int(flops), int(size)),
            name=name,
        )(*args)

    SAME, INNER, OUTER = (0, 0), (1, -1), (-1, 1)

    pack = array((80, 128))
    keep, give = call(
        give_kernel, "give", [pack, pack], [core_s, conv_weight, proj_weight], 1e5, 1e5, [pltpu.VMEM((80, 128), F32)]
    )
    got = send(give, 0, INNER)
    (spread,) = call(
        spread_kernel,
        "spread",
        [array((64, 152, 128))],
        [core_s, keep, got],
        1e5,
        3e6,
        [pltpu.VMEM((152, 128), F32), pltpu.VMEM((8, 152, 128), BF), pltpu.SemaphoreType.DMA((8,))],
        limit=40 * 1024 * 1024,
    )
    mine = lax.all_to_all(spread, CHIPS, 0, 0)
    (ft,) = call(flip_kernel, "flip", [array((1024, 1536))], [features], 1e6, 6e6)
    mine, ft = lax.optimization_barrier((mine, ft))
    other = send(mine, 0, INNER)
    (proj,) = call(rows_kernel, "rows", [array((256, 256))], [core_s, mine], 1e6, 1e6, [pltpu.VMEM((256, 256), F32)])
    other, proj = lax.optimization_barrier((other, proj))
    tile, strip, small, side = (32, 48, 256), (16, 48, 256), (16, 16, 256), (32, 16, 256)
    n, s, inner, outer, cn, cs = call(
        halo_kernel,
        "halo",
        [array(strip), array(strip), array((64, 16, 256)), array(side), array(small), array(small)],
        [core_s, features, mine, other],
        3.5e9,
        9e6,
        [pltpu.VMEM((2, 64, 16, 256), BF), pltpu.VMEM((16, 80, 256), F32)],
    )
    inner = send(inner, 0, INNER)
    n, s = call(merge_kernel, "merge", [array(strip), array(strip)], [core_s, n, s, inner], 1e6, 2e6)
    from_s = send(n, -1, SAME)
    from_n = send(s, 1, SAME)
    outer = send(outer, 0, OUTER)
    corner_s = send(cn, -1, OUTER)
    corner_n = send(cs, 1, OUTER)

    own, hg = call(
        own_kernel,
        "own",
        [array(tile, F32), array(tile, F32)],
        [core_s, features, mine, other, cotangent, proj, conv_bias.reshape(1, 256)],
        4e9,
        12e6,
    )
    hidden, g_top, g_low, gi, go, ct, cl = call(
        point_kernel,
        "point",
        [array(tile), array(strip), array(strip), array(side), array(side), array(small), array(small)],
        [core_s, own, hg, from_n, from_s, inner, outer, corner_n, corner_s],
        1e8,
        6e6,
        [pltpu.VMEM(tile, F32)],
    )

    h_top = send(g_low, 1, SAME)
    h_low = send(g_top, -1, SAME)
    h_outer = send(go, 0, OUTER)
    c_top = send(cl, 1, OUTER)
    c_low = send(ct, -1, OUTER)
    h_inner = send(gi, 0, INNER)

    ends = array((64, 8, 128))
    projected, e_mine, e_other = call(
        proj_kernel,
        "proj",
        [array(tile), ends, ends],
        [core_s, hidden, cotangent, proj, g_top, g_low],
        4e9,
        4e6,
        [pltpu.VMEM((256, 256), F32), pltpu.VMEM((64, 8, 128), F32)],
    )
    part = array((3072, 128))
    g_mid, m1, o1 = call(
        wgrad_mid_kernel,
        "wgrad1",
        [array((32, 80, 256)), part, part],
        [core_s, ft, g_top, g_low, h_inner, h_outer],
        2.4e9,
        6e6,
    )
    r1 = send(o1, 0, INNER)
    h_top, h_low, c_top, c_low, e_mine, e_other, m1 = lax.optimization_barrier(
        (h_top, h_low, c_top, c_low, e_mine, e_other, m1)
    )
    (edge,) = call(edge_kernel, "edge", [array(side)], [core_s, h_top, h_low], 1e6, 1e6)
    edge = send(edge, 0, INNER)
    row, long = array((16, 80, 256)), array((3584, 128))
    g_bottom, m0, o0 = call(
        functools.partial(wgrad_row_kernel, 0),
        "wgrad0",
        [row, part, long],
        [core_s, ft, g_mid, h_low, c_low, edge, e_other],
        2.4e9,
        6e6,
    )
    r0 = send(o0, 0, INNER)
    g_upper, m2, o2 = call(
        functools.partial(wgrad_row_kernel, 2),
        "wgrad2",
        [row, part, part],
        [core_s, ft, g_mid, h_top, c_top, edge, e_mine],
        2.4e9,
        6e6,
    )
    r2 = send(o2, 0, INNER)
    (t1,) = call(add_kernel, "add1", [part], [m1, r1], 1e6, 4e6)
    (t0,) = call(add_kernel, "add0", [part], [m0, r0], 1e6, 4e6)
    (total,) = call(
        gather_kernel,
        "gather",
        [array((64, 152, 128))],
        [t0, t1, m2, r2, e_mine, r0, spread],
        1e6,
        7e6,
        [pltpu.VMEM((64, 152, 128), BF), pltpu.SemaphoreType.DMA((8,))],
        far=(spread,),
        reuse=6,
    )
    pieces = lax.all_to_all(total, CHIPS, 0, 0)

    (features_grad,) = call(
        fgrad_kernel, "fgrad", [array((32, 48, 1024))], [g_upper, g_mid, g_bottom, mine, other], 7.2e9, 12e6
    )

    pack = array((80, 128), F32)
    keep, give, bias_row = call(
        sum_kernel,
        "sum",
        [pack, pack, array((1, 128), F32)],
        [core_s, pieces],
        1e6,
        3e6,
        [pltpu.VMEM((152, 128), F32), pltpu.VMEM((64, 152, 128), BF), pltpu.SemaphoreType.DMA((4,))],
        far=(pieces,),
    )
    got = send(give, 0, INNER)
    conv_grad, proj_grad = call(
        join_kernel, "join", [array((72, 256), F32), array((2, 256), F32)], [core_s, keep, got], 1e5, 1e5
    )
    here = 2 * lax.axis_index(ALL) % 128
    bias_grad = lax.dynamic_slice(bias_row.reshape(128), (here,), (2,))
    return projected, features_grad, conv_grad, proj_grad, bias_grad


def solution(mesh):
    fine = Mesh(mesh.devices.reshape(4, 4, 4, 2), ALL)
    tile = P(("y", "x"), ("z", "core"), None)
    rows = P(ALL, None)
    return jax.shard_map(
        body,
        mesh=fine,
        in_specs=(tile, rows, P(), rows, tile),
        out_specs=(tile, tile, rows, rows, P(ALL)),
        check_vma=False,
    )
```

```python
import functools

import jax
import jax.numpy as jnp
import numpy as np
from jax import lax
from jax.experimental import pallas as pl
from jax.experimental.pallas import tpu as pltpu
from jax.sharding import Mesh, PartitionSpec as P

D = 16
CHIPS = ("y", "x", "z")
ALL = ("y", "x", "z", "core")
BF = jnp.bfloat16
F32 = jnp.float32
VMEM_LIMIT = 18 * 1024 * 1024

NN = (((1,), (0,)), ((), ()))
NT = (((1,), (1,)), ((), ()))
TN = (((0,), (0,)), ((), ()))


def dot(a, b, dims=NN):
    return lax.dot_general(a, b, dims, preferred_element_type=F32)


def vmem():
    return pl.BlockSpec(memory_space=pltpu.VMEM)


def any_space():
    return pl.BlockSpec(memory_space=pl.ANY)


def params(limit):
    return pltpu.CompilerParams(vmem_limit_bytes=limit)


def cost(flops, size):
    return pl.CostEstimate(flops=flops, bytes_accessed=size, transcendentals=0)


def swap(x):
    return jnp.concatenate([x[..., 128:], x[..., :128]], axis=-1)


def tap(mine_ref, other_ref, a, b):
    row = (3 * a + b) * 1024
    first, last = row // 144, -(-(row + 1024) // 144)
    skip = row - 144 * first

    def half(ref):
        return ref[first:last, 0:144, :].reshape((last - first) * 144, 128)[skip : skip + 1024]

    return jnp.concatenate([half(mine_ref), half(other_ref)], axis=1)


def px(ref, r0, r1, c0, c1):
    return ref[r0:r1, c0:c1, :].reshape((r1 - r0) * (c1 - c0), ref.shape[2])


def give_kernel(core_ref, conv_ref, proj_ref, keep_ref, give_ref, acc):
    first = core_ref[0] == 0
    low, high = conv_ref[:, :128].astype(F32), conv_ref[:, 128:].astype(F32)
    proj = proj_ref[...].astype(F32)
    acc[...] = jnp.zeros_like(acc)
    acc[72:74] = proj[:, :128]
    acc[74:76] = proj[:, 128:]
    acc[0:72] = jnp.where(first, low, high)
    keep_ref[...] = acc[...].astype(BF)
    acc[0:72] = jnp.where(first, high, low)
    give_ref[...] = acc[...].astype(BF)


def spread_kernel(core_ref, keep_ref, got_ref, out_ref, acc, many, sems):
    first = core_ref[0] == 0
    keep, got = keep_ref[...].astype(F32), got_ref[...].astype(F32)
    even, odd = jnp.where(first, keep, got), jnp.where(first, got, keep)
    acc[0:72] = even[0:72]
    acc[72:144] = odd[0:72]
    acc[144:146] = even[72:74]
    acc[146:148] = odd[72:74]
    acc[148:150] = even[74:76]
    acc[150:152] = odd[74:76]
    chunk = acc[...].astype(BF)
    for k in range(8):
        many[k] = chunk
    copies = [pltpu.make_async_copy(many, out_ref.at[pl.ds(8 * k, 8)], sems.at[k]) for k in range(8)]
    for copy in copies:
        copy.start()
    for copy in copies:
        copy.wait()


def flip_kernel(f_ref, ft_ref):
    for k in range(6):
        i, j = divmod(k, 3)
        block = px(f_ref, 16 * i, 16 * i + 16, 16 * j, 16 * j + 16)
        ft_ref[:, 256 * k : 256 * k + 256] = block.T


def rows_kernel(core_ref, mine_ref, proj_ref, acc):
    for k in range(64):
        x = mine_ref[k, 144:152, :].astype(F32)
        acc[4 * k : 4 * k + 4, :128] = x[0:4]
        acc[4 * k : 4 * k + 4, 128:] = x[4:8]
    start = pl.multiple_of(128 * core_ref[0], 128)
    proj_ref[0:128] = acc[pl.ds(start, 128), :].astype(BF)
    proj_ref[128:256] = acc[pl.ds(128 - start, 128), :].astype(BF)


def rows_out_kernel(core_ref, f_ref, mine_ref, other_ref, n_ref, s_ref, inner_ref, cn_ref, cs_ref, sides, acc):
    core = core_ref[0]
    for out, a, r0, block in ((n_ref, 2, 0, 0), (s_ref, 0, 16, 1)):
        acc[...] = jnp.zeros_like(acc)
        for b in range(3):
            c = (2 - b) * D
            acc[:, c : c + 48, :] += dot(px(f_ref, r0, r0 + 16, 0, 48), tap(mine_ref, other_ref, a, b)).reshape(
                16, 48, 256
            )
        sides[0, 16 * block : 16 * block + 16] = acc[:, 0:16, :].astype(BF)
        out[...] = acc[:, 16:64, :].astype(BF)
        sides[1, 16 * block : 16 * block + 16] = acc[:, 64:80, :].astype(BF)
    inner_ref[...] = sides[1 - core]
    cn_ref[...] = sides[core, 0:16]
    cs_ref[...] = sides[core, 16:32]


def sides_out_kernel(core_ref, f_ref, mine_ref, other_ref, inner_ref, outer_ref, sides):
    core = core_ref[0]
    for side, b, c0 in ((0, 2, 0), (1, 0, 32)):
        mid = dot(px(f_ref, 0, 32, c0, c0 + 16), tap(mine_ref, other_ref, 1, b))
        top = mid[:256] + dot(px(f_ref, 16, 32, c0, c0 + 16), tap(mine_ref, other_ref, 2, b))
        low = mid[256:] + dot(px(f_ref, 0, 16, c0, c0 + 16), tap(mine_ref, other_ref, 0, b))
        sides[side, 0:16] = top.reshape(16, 16, 256).astype(BF)
        sides[side, 16:32] = low.reshape(16, 16, 256).astype(BF)
    inner_ref[...] = sides[1 - core]
    outer_ref[...] = sides[core]


def merge_kernel(core_ref, n_ref, s_ref, inner_ref, no_ref, so_ref):
    cols = pl.ds(pl.multiple_of(32 - 32 * core_ref[0], 16), 16)
    for src, dst, r in ((n_ref, no_ref, 0), (s_ref, so_ref, 16)):
        dst[...] = src[...]
        dst[:, cols, :] = (src[:, cols, :].astype(F32) + swap(inner_ref[r : r + 16]).astype(F32)).astype(BF)


def own_kernel(core_ref, f_ref, mine_ref, other_ref, cot_ref, proj_ref, bias_ref, pre_ref, hg_ref):
    first = dot(px(f_ref, 0, 32, 0, 48), tap(mine_ref, other_ref, 1, 1))
    bias = bias_ref[...]
    bias = jnp.where(core_ref[0] == 0, bias, swap(bias))
    pre_ref[...] = (first + bias).reshape(32, 48, 256)
    for a, rows in ((0, ((0, 16), (16, 32))), (1, ((0, 32), (0, 32))), (2, ((16, 32), (0, 16)))):
        for b, cols in ((0, ((0, 32), (16, 48))), (1, ((0, 48), (0, 48))), (2, ((16, 48), (0, 32)))):
            if a == 1 and b == 1:
                continue
            (fr, pr), (fc, pc) = rows, cols
            pre_ref[pr[0] : pr[1], pc[0] : pc[1], :] += dot(
                px(f_ref, *fr, *fc), tap(mine_ref, other_ref, a, b)
            ).reshape(pr[1] - pr[0], pc[1] - pc[0], 256)
    hg_ref[...] = dot(px(cot_ref, 0, 32, 0, 48), proj_ref[...], NT).reshape(32, 48, 256)


def point_kernel(
    core_ref, own_ref, hg_ref, n_ref, s_ref, inner_ref, outer_ref, cn_ref, cs_ref,
    hid_ref, top_ref, low_ref, gi_ref, go_ref, ct_ref, cl_ref, pre_ref,
):
    core = core_ref[0]
    inner = pl.ds(pl.multiple_of(32 - 32 * core, 16), 16)
    outer = pl.ds(pl.multiple_of(32 * core, 16), 16)
    pre_ref[0:16] = own_ref[0:16] + n_ref[...].astype(F32)
    pre_ref[16:32] = own_ref[16:32] + s_ref[...].astype(F32)
    pre_ref[:, inner, :] += swap(inner_ref[...]).astype(F32)
    pre_ref[:, outer, :] += swap(outer_ref[...]).astype(F32)
    pre_ref[0:16, outer, :] += swap(cn_ref[...]).astype(F32)
    pre_ref[16:32, outer, :] += swap(cs_ref[...]).astype(F32)
    for g_ref, base in ((top_ref, 0), (low_ref, 16)):

        @pl.loop(0, 8)
        def _(k):
            rows = pl.ds(base + 2 * k, 2)
            pre = pre_ref[rows]
            s = jax.nn.sigmoid(pre)
            hid_ref[rows] = (pre * s).astype(BF)
            g_ref[pl.ds(2 * k, 2)] = (hg_ref[rows] * s * (1.0 + pre * (1.0 - s))).astype(BF)

    for g_ref, c_ref, base in ((top_ref, ct_ref, 0), (low_ref, cl_ref, 16)):
        gi_ref[base : base + 16] = g_ref[:, inner, :]
        edge = g_ref[:, outer, :]
        go_ref[base : base + 16] = edge
        c_ref[...] = edge


def proj_kernel(core_ref, hid_ref, cot_ref, proj_ref, top_ref, low_ref, out_ref, em_ref, eo_ref, pw, ext):
    first = core_ref[0] == 0
    start = pl.multiple_of(128 * core_ref[0], 128)
    hidden = px(hid_ref, 0, 32, 0, 48)
    cot = px(cot_ref, 0, 32, 0, 48)
    out_ref[...] = dot(hidden, proj_ref[...]).astype(BF).reshape(32, 48, 256)
    term = dot(hidden, cot, TN)
    term = jnp.where(first, term, swap(term))
    pw[pl.ds(start, 128), :] = term[0:128]
    pw[pl.ds(128 - start, 128), :] = term[128:256]
    total = px(top_ref, 0, 16, 0, 48).astype(F32) + px(low_ref, 0, 16, 0, 48).astype(F32)
    bias = jnp.sum(total, axis=0, keepdims=True)
    bias = jnp.where(first, bias, swap(bias))
    for e_ref, c in ((em_ref, 0), (eo_ref, 128)):
        for k in range(64):
            ext[k, 0:4] = pw[4 * k : 4 * k + 4, c : c + 128]
            ext[k, 4:8] = jnp.broadcast_to(bias[:, 128 * (k // 32) : 128 * (k // 32) + 128], (4, 128))
        e_ref[...] = ext[...].astype(BF)


def edge_kernel(core_ref, top_ref, low_ref, edge_ref):
    cols = pl.ds(pl.multiple_of(32 - 32 * core_ref[0], 16), 16)
    edge_ref[0:16] = top_ref[:, cols, :]
    edge_ref[16:32] = low_ref[:, cols, :]


def wgrad_taps(ft_ref, block, a, mine_ref, other_ref):
    for b in range(3):
        blocks = [block(i, 2 - b + j) for i in range(2) for j in range(3)]
        res = dot(ft_ref[...], jnp.concatenate(blocks, axis=0)).astype(BF)
        mine_ref[1024 * b : 1024 * b + 1024] = res[:, :128]
        other_ref[1024 * b : 1024 * b + 1024] = res[:, 128:]


def wgrad_mid_kernel(core_ref, ft_ref, gt_ref, gl_ref, hi_ref, ho_ref, g_ref, mine_ref, other_ref):
    core = core_ref[0]
    inner = pl.ds(pl.multiple_of(64 - 64 * core, 16), 16)
    outer = pl.ds(pl.multiple_of(64 * core, 16), 16)
    g_ref[0:16, 16:64, :] = gt_ref[...]
    g_ref[16:32, 16:64, :] = gl_ref[...]
    g_ref[:, inner, :] = swap(hi_ref[...])
    g_ref[:, outer, :] = swap(ho_ref[...])
    wgrad_taps(
        ft_ref, lambda i, j: px(g_ref, 16 * i, 16 * i + 16, 16 * j, 16 * j + 16), 1, mine_ref, other_ref
    )


def wgrad_row_kernel(a, core_ref, ft_ref, g_ref, h_ref, c_ref, edge_ref, e_ref, row_ref, mine_ref, other_ref):
    core = core_ref[0]
    row_ref[:, 16:64, :] = h_ref[...]
    row_ref[:, pl.ds(pl.multiple_of(64 - 64 * core, 16), 16), :] = swap(edge_ref[8 * (2 - a) : 8 * (2 - a) + 16])
    row_ref[:, pl.ds(pl.multiple_of(64 * core, 16), 16), :] = swap(c_ref[...])

    def block(i, j):
        if a == 0:
            return px(g_ref, 16, 32, 16 * j, 16 * j + 16) if i == 0 else px(row_ref, 0, 16, 16 * j, 16 * j + 16)
        return px(g_ref, 0, 16, 16 * j, 16 * j + 16) if i == 1 else px(row_ref, 0, 16, 16 * j, 16 * j + 16)

    wgrad_taps(ft_ref, block, a, mine_ref, other_ref)
    if a == 0:
        other_ref[3072:3584] = e_ref[...].reshape(512, 128)


def add_kernel(m_ref, r_ref, out_ref):
    @pl.loop(0, 12)
    def _(k):
        rows = pl.ds(pl.multiple_of(256 * k, 256), 256)
        out_ref[rows] = (m_ref[rows].astype(F32) + r_ref[rows].astype(F32)).astype(BF)


def gather_kernel(t0_ref, t1_ref, m2_ref, r2_ref, e_ref, r0_ref, out_ref, near, sems):
    copies = []
    for k in range(64):
        at = 144 * k
        while at < 144 * (k + 1):
            part, row = divmod(at, 3072)
            size = min(144 * (k + 1) - at, 3072 - row)
            if part < 2:
                value = (t0_ref, t1_ref)[part][row : row + size]
            else:
                value = (m2_ref[row : row + size].astype(F32) + r2_ref[row : row + size].astype(F32)).astype(BF)
            near[k, at - 144 * k : at - 144 * k + size] = value
            at += size
        ends = e_ref[k].astype(F32) + r0_ref[3072 + 8 * k : 3080 + 8 * k].astype(F32)
        near[k, 144:152] = ends.astype(BF)
        if k % 8 == 7:
            part = pl.ds(k - 7, 8)
            copy = pltpu.make_async_copy(near.at[part], out_ref.at[part], sems.at[k // 8])
            copy.start()
            copies.append(copy)
    for copy in copies:
        copy.wait()


def sum_kernel(core_ref, far_ref, keep_ref, give_ref, bias_ref, acc, near, sems):
    copies = [
        pltpu.make_async_copy(far_ref.at[pl.ds(16 * k, 16)], near.at[pl.ds(16 * k, 16)], sems.at[k]) for k in range(4)
    ]
    for copy in copies:
        copy.start()
    total = jnp.zeros((152, 128), F32)
    for k, copy in enumerate(copies):
        copy.wait()
        total = lax.fori_loop(16 * k, 16 * k + 16, lambda n, t: t + near[n].astype(F32), total, unroll=4)
    acc[...] = total
    bias_ref[...] = acc[148:149]
    for out, c in ((keep_ref, core_ref[0]), (give_ref, 1 - core_ref[0])):
        out[0:72] = acc[pl.ds(pl.multiple_of(72 * c, 8), 72)]
        out[72:80] = jnp.where(c == 0, acc[144:152], pltpu.roll(acc[144:152], 6, 0))


def join_kernel(core_ref, keep_ref, got_ref, conv_ref, proj_ref):
    first = core_ref[0] == 0
    keep, got = keep_ref[...], got_ref[...]
    both = jnp.concatenate([jnp.where(first, keep, got), jnp.where(first, got, keep)], axis=1)
    conv_ref[...] = both[0:72]
    proj_ref[...] = both[72:74]


def fgrad_kernel(top_ref, mid_ref, low_ref, mine_ref, other_ref, out_ref):
    for k in range(4):
        acc = None
        for a in range(3):
            row = 8 * k + (2 - a) * 16
            ref, row = ((top_ref, row), (mid_ref, row - 16), (mid_ref, row - 16), (low_ref, row - 48))[row // 16]
            for b in range(3):
                win = px(ref, row, row + 8, (2 - b) * D, (2 - b) * D + 48)
                term = dot(win, tap(mine_ref, other_ref, a, b), NT)
                acc = term if acc is None else acc + term
        out_ref[8 * k : 8 * k + 8] = acc.astype(BF).reshape(8, 48, 1024)


def body(features, conv_weight, conv_bias, proj_weight, cotangent):
    core = lax.axis_index("core")
    core_s = core.astype(jnp.int32).reshape(1)
    smem = pl.BlockSpec(memory_space=pltpu.SMEM)

    def send(x, dr, dc):
        perm = []
        for i in range(128):
            r, c = i // 8 + dr, i % 8 + dc[i % 2]
            if 0 <= r < 16 and 0 <= c < 8:
                perm.append((i, r * 8 + c))
        return lax.ppermute(x, ALL, perm)

    def array(shape, dtype=BF):
        return jax.ShapeDtypeStruct(shape, dtype)

    def call(kernel, name, outs, args, flops, size, scratch=(), far=(), limit=VMEM_LIMIT, reuse=None):
        specs = [smem if a is core_s else any_space() if any(a is f for f in far) else vmem() for a in args]
        return pl.pallas_call(
            kernel,
            out_shape=tuple(outs),
            in_specs=specs,
            out_specs=((vmem() if limit == VMEM_LIMIT and reuse is None else any_space()),) * len(outs),
            scratch_shapes=list(scratch),
            input_output_aliases={} if reuse is None else {reuse: 0},
            compiler_params=params(limit),
            cost_estimate=cost(int(flops), int(size)),
            name=name,
        )(*args)

    SAME, INNER, OUTER = (0, 0), (1, -1), (-1, 1)

    pack = array((80, 128))
    keep, give = call(
        give_kernel, "give", [pack, pack], [core_s, conv_weight, proj_weight], 1e5, 1e5, [pltpu.VMEM((80, 128), F32)]
    )
    got = send(give, 0, INNER)
    (spread,) = call(
        spread_kernel,
        "spread",
        [array((64, 152, 128))],
        [core_s, keep, got],
        1e5,
        3e6,
        [pltpu.VMEM((152, 128), F32), pltpu.VMEM((8, 152, 128), BF), pltpu.SemaphoreType.DMA((8,))],
        limit=40 * 1024 * 1024,
    )
    mine = lax.all_to_all(spread, CHIPS, 0, 0)
    mine, features = lax.optimization_barrier((mine, features))
    (ft,) = call(flip_kernel, "flip", [array((1024, 1536))], [features], 1e9, 6e6)
    other = send(mine, 0, INNER)
    (proj,) = call(rows_kernel, "rows", [array((256, 256))], [core_s, mine], 1e6, 1e6, [pltpu.VMEM((256, 256), F32)])
    other, proj, ft = lax.optimization_barrier((other, proj, ft))
    tile, strip, small, side = (32, 48, 256), (16, 48, 256), (16, 16, 256), (32, 16, 256)
    n, s, corners, cn, cs = call(
        rows_out_kernel,
        "rows_out",
        [array(strip), array(strip), array(side), array(small), array(small)],
        [core_s, features, mine, other],
        1.7e9,
        9e6,
        [pltpu.VMEM((2, 32, 16, 256), BF), pltpu.VMEM((16, 80, 256), F32)],
    )
    corners, features = lax.optimization_barrier((corners, features))
    corners = send(corners, 0, INNER)
    inner, outer = call(
        sides_out_kernel,
        "sides_out",
        [array(side), array(side)],
        [core_s, features, mine, other],
        1.9e9,
        9e6,
        [pltpu.VMEM((2, 32, 16, 256), BF)],
    )
    n, inner = lax.optimization_barrier((n, inner))
    n, s = call(merge_kernel, "merge", [array(strip), array(strip)], [core_s, n, s, corners], 1e6, 2e6)
    inner = send(inner, 0, INNER)
    from_s = send(n, -1, SAME)
    from_n = send(s, 1, SAME)
    outer = send(outer, 0, OUTER)
    corner_s = send(cn, -1, OUTER)
    corner_n = send(cs, 1, OUTER)

    own, hg = call(
        own_kernel,
        "own",
        [array(tile, F32), array(tile, F32)],
        [core_s, features, mine, other, cotangent, proj, conv_bias.reshape(1, 256)],
        4e9,
        12e6,
    )
    hidden, g_top, g_low, gi, go, ct, cl = call(
        point_kernel,
        "point",
        [array(tile), array(strip), array(strip), array(side), array(side), array(small), array(small)],
        [core_s, own, hg, from_n, from_s, inner, outer, corner_n, corner_s],
        1e8,
        6e6,
        [pltpu.VMEM(tile, F32)],
    )

    h_top = send(g_low, 1, SAME)
    h_low = send(g_top, -1, SAME)
    h_outer = send(go, 0, OUTER)
    c_top = send(cl, 1, OUTER)
    c_low = send(ct, -1, OUTER)
    h_inner = send(gi, 0, INNER)

    part = array((3072, 128))
    g_mid, m1, o1 = call(
        wgrad_mid_kernel,
        "wgrad1",
        [array((32, 80, 256)), part, part],
        [core_s, ft, g_top, g_low, h_inner, h_outer],
        1e8,
        6e6,
    )
    r1 = send(o1, 0, INNER)
    hidden, m1 = lax.optimization_barrier((hidden, m1))
    ends = array((64, 8, 128))
    projected, e_mine, e_other = call(
        proj_kernel,
        "proj",
        [array(tile), ends, ends],
        [core_s, hidden, cotangent, proj, g_top, g_low],
        1e8,
        4e6,
        [pltpu.VMEM((256, 256), F32), pltpu.VMEM((64, 8, 128), F32)],
    )
    h_top, h_low, c_top, c_low, e_mine, e_other, m1 = lax.optimization_barrier(
        (h_top, h_low, c_top, c_low, e_mine, e_other, m1)
    )
    (edge,) = call(edge_kernel, "edge", [array(side)], [core_s, h_top, h_low], 1e6, 1e6)
    edge = send(edge, 0, INNER)
    row, long = array((16, 80, 256)), array((3584, 128))
    g_bottom, m0, o0 = call(
        functools.partial(wgrad_row_kernel, 0),
        "wgrad0",
        [row, part, long],
        [core_s, ft, g_mid, h_low, c_low, edge, e_other],
        2.4e9,
        6e6,
    )
    r0 = send(o0, 0, INNER)
    g_upper, m2, o2 = call(
        functools.partial(wgrad_row_kernel, 2),
        "wgrad2",
        [row, part, part],
        [core_s, ft, g_mid, h_top, c_top, edge, e_mine],
        2.4e9,
        6e6,
    )
    r2 = send(o2, 0, INNER)
    (t1,) = call(add_kernel, "add1", [part], [m1, r1], 1e6, 4e6)
    (t0,) = call(add_kernel, "add0", [part], [m0, r0], 1e6, 4e6)
    (total,) = call(
        gather_kernel,
        "gather",
        [array((64, 152, 128))],
        [t0, t1, m2, r2, e_mine, r0],
        1e6,
        7e6,
        [pltpu.VMEM((64, 152, 128), BF), pltpu.SemaphoreType.DMA((8,))],
        limit=49 * 1024 * 1024,
    )
    pieces = lax.all_to_all(total, CHIPS, 0, 0)

    (features_grad,) = call(
        fgrad_kernel, "fgrad", [array((32, 48, 1024))], [g_upper, g_mid, g_bottom, mine, other], 7.2e9, 12e6
    )

    pack = array((80, 128), F32)
    keep, give, bias_row = call(
        sum_kernel,
        "sum",
        [pack, pack, array((1, 128), F32)],
        [core_s, pieces],
        1e6,
        3e6,
        [pltpu.VMEM((152, 128), F32), pltpu.VMEM((64, 152, 128), BF), pltpu.SemaphoreType.DMA((4,))],
        far=(pieces,),
    )
    got = send(give, 0, INNER)
    conv_grad, proj_grad = call(
        join_kernel, "join", [array((72, 256), F32), array((2, 256), F32)], [core_s, keep, got], 1e5, 1e5
    )
    here = 2 * lax.axis_index(ALL) % 128
    bias_grad = lax.dynamic_slice(bias_row.reshape(128), (here,), (2,))
    return projected, features_grad, conv_grad, proj_grad, bias_grad


def solution(mesh):
    fine = Mesh(mesh.devices.reshape(4, 4, 4, 2), ALL)
    tile = P(("y", "x"), ("z", "core"), None)
    rows = P(ALL, None)
    return jax.shard_map(
        body,
        mesh=fine,
        in_specs=(tile, rows, P(), rows, tile),
        out_specs=(tile, tile, rows, rows, P(ALL)),
        check_vma=False,
    )
```

```python
import functools

import jax
import jax.numpy as jnp
import numpy as np
from jax import lax
from jax.experimental import pallas as pl
from jax.experimental.pallas import tpu as pltpu
from jax.sharding import Mesh, PartitionSpec as P

D = 16
CHIPS = ("y", "x", "z")
ALL = ("y", "x", "z", "core")
BF = jnp.bfloat16
F32 = jnp.float32
VMEM_LIMIT = 18 * 1024 * 1024

NN = (((1,), (0,)), ((), ()))
NT = (((1,), (1,)), ((), ()))
TN = (((0,), (0,)), ((), ()))


def dot(a, b, dims=NN):
    return lax.dot_general(a, b, dims, preferred_element_type=F32)


def vmem():
    return pl.BlockSpec(memory_space=pltpu.VMEM)


def any_space():
    return pl.BlockSpec(memory_space=pl.ANY)


def params(limit):
    return pltpu.CompilerParams(vmem_limit_bytes=limit)


def cost(flops, size):
    return pl.CostEstimate(flops=flops, bytes_accessed=size, transcendentals=0)


def swap(x):
    return jnp.concatenate([x[..., 128:], x[..., :128]], axis=-1)


def tap(mine_ref, other_ref, a, b):
    row = (3 * a + b) * 1024
    first, last = row // 144, -(-(row + 1024) // 144)
    skip = row - 144 * first

    def half(ref):
        return ref[first:last, 0:144, :].reshape((last - first) * 144, 128)[skip : skip + 1024]

    return jnp.concatenate([half(mine_ref), half(other_ref)], axis=1)


def px(ref, r0, r1, c0, c1):
    return ref[r0:r1, c0:c1, :].reshape((r1 - r0) * (c1 - c0), ref.shape[2])


def give_kernel(core_ref, conv_ref, proj_ref, keep_ref, give_ref, acc):
    first = core_ref[0] == 0
    low, high = conv_ref[:, :128].astype(F32), conv_ref[:, 128:].astype(F32)
    proj = proj_ref[...].astype(F32)
    acc[...] = jnp.zeros_like(acc)
    acc[72:74] = proj[:, :128]
    acc[74:76] = proj[:, 128:]
    acc[0:72] = jnp.where(first, low, high)
    keep_ref[...] = acc[...].astype(BF)
    acc[0:72] = jnp.where(first, high, low)
    give_ref[...] = acc[...].astype(BF)


def spread_kernel(core_ref, keep_ref, got_ref, out_ref, acc, many, sems):
    first = core_ref[0] == 0
    keep, got = keep_ref[...].astype(F32), got_ref[...].astype(F32)
    even, odd = jnp.where(first, keep, got), jnp.where(first, got, keep)
    acc[0:72] = even[0:72]
    acc[72:144] = odd[0:72]
    acc[144:146] = even[72:74]
    acc[146:148] = odd[72:74]
    acc[148:150] = even[74:76]
    acc[150:152] = odd[74:76]
    chunk = acc[...].astype(BF)
    for k in range(8):
        many[k] = chunk
    copies = [pltpu.make_async_copy(many, out_ref.at[pl.ds(8 * k, 8)], sems.at[k]) for k in range(8)]
    for copy in copies:
        copy.start()
    for copy in copies:
        copy.wait()


def flip_kernel(f_ref, ft_ref):
    for k in range(6):
        i, j = divmod(k, 3)
        block = px(f_ref, 16 * i, 16 * i + 16, 16 * j, 16 * j + 16)
        ft_ref[:, 256 * k : 256 * k + 256] = block.T


def rows_kernel(core_ref, mine_ref, proj_ref, acc):
    for k in range(64):
        x = mine_ref[k, 144:152, :].astype(F32)
        acc[4 * k : 4 * k + 4, :128] = x[0:4]
        acc[4 * k : 4 * k + 4, 128:] = x[4:8]
    start = pl.multiple_of(128 * core_ref[0], 128)
    proj_ref[0:128] = acc[pl.ds(start, 128), :].astype(BF)
    proj_ref[128:256] = acc[pl.ds(128 - start, 128), :].astype(BF)


def rows_out_kernel(core_ref, f_ref, mine_ref, other_ref, n_ref, s_ref, inner_ref, cn_ref, cs_ref, sides, acc):
    core = core_ref[0]
    for out, a, r0, block in ((n_ref, 2, 0, 0), (s_ref, 0, 16, 1)):
        acc[...] = jnp.zeros_like(acc)
        for b in range(3):
            c = (2 - b) * D
            acc[:, c : c + 48, :] += dot(px(f_ref, r0, r0 + 16, 0, 48), tap(mine_ref, other_ref, a, b)).reshape(
                16, 48, 256
            )
        sides[0, 16 * block : 16 * block + 16] = acc[:, 0:16, :].astype(BF)
        out[...] = acc[:, 16:64, :].astype(BF)
        sides[1, 16 * block : 16 * block + 16] = acc[:, 64:80, :].astype(BF)
    inner_ref[...] = sides[1 - core]
    cn_ref[...] = sides[core, 0:16]
    cs_ref[...] = sides[core, 16:32]


def sides_out_kernel(core_ref, f_ref, mine_ref, other_ref, inner_ref, outer_ref, sides):
    core = core_ref[0]
    for side, b, c0 in ((0, 2, 0), (1, 0, 32)):
        mid = dot(px(f_ref, 0, 32, c0, c0 + 16), tap(mine_ref, other_ref, 1, b))
        top = mid[:256] + dot(px(f_ref, 16, 32, c0, c0 + 16), tap(mine_ref, other_ref, 2, b))
        low = mid[256:] + dot(px(f_ref, 0, 16, c0, c0 + 16), tap(mine_ref, other_ref, 0, b))
        sides[side, 0:16] = top.reshape(16, 16, 256).astype(BF)
        sides[side, 16:32] = low.reshape(16, 16, 256).astype(BF)
    inner_ref[...] = sides[1 - core]
    outer_ref[...] = sides[core]


def merge_kernel(core_ref, n_ref, s_ref, inner_ref, no_ref, so_ref):
    cols = pl.ds(pl.multiple_of(32 - 32 * core_ref[0], 16), 16)
    for src, dst, r in ((n_ref, no_ref, 0), (s_ref, so_ref, 16)):
        dst[...] = src[...]
        dst[:, cols, :] = (src[:, cols, :].astype(F32) + swap(inner_ref[r : r + 16]).astype(F32)).astype(BF)


def own_kernel(core_ref, f_ref, mine_ref, other_ref, cot_ref, proj_ref, bias_ref, pre_ref, hg_ref):
    first = dot(px(f_ref, 0, 32, 0, 48), tap(mine_ref, other_ref, 1, 1))
    bias = bias_ref[...]
    bias = jnp.where(core_ref[0] == 0, bias, swap(bias))
    pre_ref[...] = (first + bias).reshape(32, 48, 256)
    for a, rows in ((0, ((0, 16), (16, 32))), (1, ((0, 32), (0, 32))), (2, ((16, 32), (0, 16)))):
        for b, cols in ((0, ((0, 32), (16, 48))), (1, ((0, 48), (0, 48))), (2, ((16, 48), (0, 32)))):
            if a == 1 and b == 1:
                continue
            (fr, pr), (fc, pc) = rows, cols
            pre_ref[pr[0] : pr[1], pc[0] : pc[1], :] += dot(
                px(f_ref, *fr, *fc), tap(mine_ref, other_ref, a, b)
            ).reshape(pr[1] - pr[0], pc[1] - pc[0], 256)
    hg_ref[...] = dot(px(cot_ref, 0, 32, 0, 48), proj_ref[...], NT).reshape(32, 48, 256)


def point_kernel(
    core_ref, own_ref, hg_ref, n_ref, s_ref, inner_ref, outer_ref, cn_ref, cs_ref,
    hid_ref, top_ref, low_ref, gi_ref, go_ref, ct_ref, cl_ref, pre_ref,
):
    core = core_ref[0]
    inner = pl.ds(pl.multiple_of(32 - 32 * core, 16), 16)
    outer = pl.ds(pl.multiple_of(32 * core, 16), 16)
    pre_ref[0:16] = own_ref[0:16] + n_ref[...].astype(F32)
    pre_ref[16:32] = own_ref[16:32] + s_ref[...].astype(F32)
    pre_ref[:, inner, :] += swap(inner_ref[...]).astype(F32)
    pre_ref[:, outer, :] += swap(outer_ref[...]).astype(F32)
    pre_ref[0:16, outer, :] += swap(cn_ref[...]).astype(F32)
    pre_ref[16:32, outer, :] += swap(cs_ref[...]).astype(F32)
    for g_ref, base in ((top_ref, 0), (low_ref, 16)):

        @pl.loop(0, 8)
        def _(k):
            rows = pl.ds(base + 2 * k, 2)
            pre = pre_ref[rows]
            s = jax.nn.sigmoid(pre)
            hid_ref[rows] = (pre * s).astype(BF)
            g_ref[pl.ds(2 * k, 2)] = (hg_ref[rows] * s * (1.0 + pre * (1.0 - s))).astype(BF)

    for g_ref, c_ref, base in ((top_ref, ct_ref, 0), (low_ref, cl_ref, 16)):
        gi_ref[base : base + 16] = g_ref[:, inner, :]
        edge = g_ref[:, outer, :]
        go_ref[base : base + 16] = edge
        c_ref[...] = edge


def proj_kernel(core_ref, hid_ref, cot_ref, proj_ref, top_ref, low_ref, out_ref, em_ref, eo_ref, pw, ext):
    first = core_ref[0] == 0
    start = pl.multiple_of(128 * core_ref[0], 128)
    hidden = px(hid_ref, 0, 32, 0, 48)
    cot = px(cot_ref, 0, 32, 0, 48)
    out_ref[...] = dot(hidden, proj_ref[...]).astype(BF).reshape(32, 48, 256)
    term = dot(hidden, cot, TN)
    term = jnp.where(first, term, swap(term))
    pw[pl.ds(start, 128), :] = term[0:128]
    pw[pl.ds(128 - start, 128), :] = term[128:256]
    total = px(top_ref, 0, 16, 0, 48).astype(F32) + px(low_ref, 0, 16, 0, 48).astype(F32)
    bias = jnp.sum(total, axis=0, keepdims=True)
    bias = jnp.where(first, bias, swap(bias))
    for e_ref, c in ((em_ref, 0), (eo_ref, 128)):
        for k in range(64):
            ext[k, 0:4] = pw[4 * k : 4 * k + 4, c : c + 128]
            ext[k, 4:8] = jnp.broadcast_to(bias[:, 128 * (k // 32) : 128 * (k // 32) + 128], (4, 128))
        e_ref[...] = ext[...].astype(BF)


def edge_kernel(core_ref, top_ref, low_ref, edge_ref):
    cols = pl.ds(pl.multiple_of(32 - 32 * core_ref[0], 16), 16)
    edge_ref[0:16] = top_ref[:, cols, :]
    edge_ref[16:32] = low_ref[:, cols, :]


def wgrad_taps(ft_ref, block, a, mine_ref, other_ref):
    for b in range(3):
        blocks = [block(i, 2 - b + j) for i in range(2) for j in range(3)]
        res = dot(ft_ref[...], jnp.concatenate(blocks, axis=0)).astype(BF)
        mine_ref[1024 * b : 1024 * b + 1024] = res[:, :128]
        other_ref[1024 * b : 1024 * b + 1024] = res[:, 128:]


def wgrad_mid_kernel(core_ref, ft_ref, gt_ref, gl_ref, hi_ref, ho_ref, g_ref, mine_ref, other_ref):
    core = core_ref[0]
    inner = pl.ds(pl.multiple_of(64 - 64 * core, 16), 16)
    outer = pl.ds(pl.multiple_of(64 * core, 16), 16)
    g_ref[0:16, 16:64, :] = gt_ref[...]
    g_ref[16:32, 16:64, :] = gl_ref[...]
    g_ref[:, inner, :] = swap(hi_ref[...])
    g_ref[:, outer, :] = swap(ho_ref[...])
    wgrad_taps(
        ft_ref, lambda i, j: px(g_ref, 16 * i, 16 * i + 16, 16 * j, 16 * j + 16), 1, mine_ref, other_ref
    )


def wgrad_row_kernel(a, core_ref, ft_ref, g_ref, h_ref, c_ref, edge_ref, e_ref, row_ref, mine_ref, other_ref):
    core = core_ref[0]
    row_ref[:, 16:64, :] = h_ref[...]
    row_ref[:, pl.ds(pl.multiple_of(64 - 64 * core, 16), 16), :] = swap(edge_ref[8 * (2 - a) : 8 * (2 - a) + 16])
    row_ref[:, pl.ds(pl.multiple_of(64 * core, 16), 16), :] = swap(c_ref[...])

    def block(i, j):
        if a == 0:
            return px(g_ref, 16, 32, 16 * j, 16 * j + 16) if i == 0 else px(row_ref, 0, 16, 16 * j, 16 * j + 16)
        return px(g_ref, 0, 16, 16 * j, 16 * j + 16) if i == 1 else px(row_ref, 0, 16, 16 * j, 16 * j + 16)

    wgrad_taps(ft_ref, block, a, mine_ref, other_ref)
    if a == 0:
        other_ref[3072:3584] = e_ref[...].reshape(512, 128)


def add_kernel(m_ref, r_ref, out_ref):
    @pl.loop(0, 12)
    def _(k):
        rows = pl.ds(pl.multiple_of(256 * k, 256), 256)
        out_ref[rows] = (m_ref[rows].astype(F32) + r_ref[rows].astype(F32)).astype(BF)


def gather_kernel(t0_ref, t1_ref, m2_ref, r2_ref, e_ref, r0_ref, out_ref, near, sems):
    copies = []
    for k in range(64):
        at = 144 * k
        while at < 144 * (k + 1):
            part, row = divmod(at, 3072)
            size = min(144 * (k + 1) - at, 3072 - row)
            if part < 2:
                value = (t0_ref, t1_ref)[part][row : row + size]
            else:
                value = (m2_ref[row : row + size].astype(F32) + r2_ref[row : row + size].astype(F32)).astype(BF)
            near[k, at - 144 * k : at - 144 * k + size] = value
            at += size
        ends = e_ref[k].astype(F32) + r0_ref[3072 + 8 * k : 3080 + 8 * k].astype(F32)
        near[k, 144:152] = ends.astype(BF)
        if k % 8 == 7:
            part = pl.ds(k - 7, 8)
            copy = pltpu.make_async_copy(near.at[part], out_ref.at[part], sems.at[k // 8])
            copy.start()
            copies.append(copy)
    for copy in copies:
        copy.wait()


def sum_kernel(core_ref, far_ref, keep_ref, give_ref, bias_ref, acc, near, sems):
    copies = [
        pltpu.make_async_copy(far_ref.at[pl.ds(16 * k, 16)], near.at[pl.ds(16 * k, 16)], sems.at[k]) for k in range(4)
    ]
    for copy in copies:
        copy.start()
    total = jnp.zeros((152, 128), F32)
    for k, copy in enumerate(copies):
        copy.wait()
        total = lax.fori_loop(16 * k, 16 * k + 16, lambda n, t: t + near[n].astype(F32), total, unroll=4)
    acc[...] = total
    bias_ref[...] = acc[148:149]
    for out, c in ((keep_ref, core_ref[0]), (give_ref, 1 - core_ref[0])):
        out[0:72] = acc[pl.ds(pl.multiple_of(72 * c, 8), 72)]
        out[72:80] = jnp.where(c == 0, acc[144:152], pltpu.roll(acc[144:152], 6, 0))


def join_kernel(core_ref, keep_ref, got_ref, conv_ref, proj_ref):
    first = core_ref[0] == 0
    keep, got = keep_ref[...], got_ref[...]
    both = jnp.concatenate([jnp.where(first, keep, got), jnp.where(first, got, keep)], axis=1)
    conv_ref[...] = both[0:72]
    proj_ref[...] = both[72:74]


def fgrad_kernel(top_ref, mid_ref, low_ref, mine_ref, other_ref, out_ref):
    for k in range(4):
        acc = None
        for a in range(3):
            row = 8 * k + (2 - a) * 16
            ref, row = ((top_ref, row), (mid_ref, row - 16), (mid_ref, row - 16), (low_ref, row - 48))[row // 16]
            for b in range(3):
                win = px(ref, row, row + 8, (2 - b) * D, (2 - b) * D + 48)
                term = dot(win, tap(mine_ref, other_ref, a, b), NT)
                acc = term if acc is None else acc + term
        out_ref[8 * k : 8 * k + 8] = acc.astype(BF).reshape(8, 48, 1024)


def body(features, conv_weight, conv_bias, proj_weight, cotangent):
    core = lax.axis_index("core")
    core_s = core.astype(jnp.int32).reshape(1)
    smem = pl.BlockSpec(memory_space=pltpu.SMEM)

    def send(x, dr, dc):
        perm = []
        for i in range(128):
            r, c = i // 8 + dr, i % 8 + dc[i % 2]
            if 0 <= r < 16 and 0 <= c < 8:
                perm.append((i, r * 8 + c))
        return lax.ppermute(x, ALL, perm)

    def array(shape, dtype=BF):
        return jax.ShapeDtypeStruct(shape, dtype)

    def call(kernel, name, outs, args, flops, size, scratch=(), far=(), limit=VMEM_LIMIT, reuse=None):
        specs = [smem if a is core_s else any_space() if any(a is f for f in far) else vmem() for a in args]
        return pl.pallas_call(
            kernel,
            out_shape=tuple(outs),
            in_specs=specs,
            out_specs=((vmem() if limit == VMEM_LIMIT and reuse is None else any_space()),) * len(outs),
            scratch_shapes=list(scratch),
            input_output_aliases={} if reuse is None else {reuse: 0},
            compiler_params=params(limit),
            cost_estimate=cost(int(flops), int(size)),
            name=name,
        )(*args)

    SAME, INNER, OUTER = (0, 0), (1, -1), (-1, 1)

    pack = array((80, 128))
    keep, give = call(
        give_kernel, "give", [pack, pack], [core_s, conv_weight, proj_weight], 1e5, 1e5, [pltpu.VMEM((80, 128), F32)]
    )
    got = send(give, 0, INNER)
    (spread,) = call(
        spread_kernel,
        "spread",
        [array((64, 152, 128))],
        [core_s, keep, got],
        1e5,
        3e6,
        [pltpu.VMEM((152, 128), F32), pltpu.VMEM((8, 152, 128), BF), pltpu.SemaphoreType.DMA((8,))],
        limit=40 * 1024 * 1024,
    )
    mine = lax.all_to_all(spread, CHIPS, 0, 0)
    mine, features = lax.optimization_barrier((mine, features))
    (ft,) = call(flip_kernel, "flip", [array((1024, 1536))], [features], 1e9, 6e6)
    other = send(mine, 0, INNER)
    (proj,) = call(rows_kernel, "rows", [array((256, 256))], [core_s, mine], 1e6, 1e6, [pltpu.VMEM((256, 256), F32)])
    other, proj, ft = lax.optimization_barrier((other, proj, ft))
    tile, strip, small, side = (32, 48, 256), (16, 48, 256), (16, 16, 256), (32, 16, 256)
    n, s, corners, cn, cs = call(
        rows_out_kernel,
        "rows_out",
        [array(strip), array(strip), array(side), array(small), array(small)],
        [core_s, features, mine, other],
        1.7e9,
        9e6,
        [pltpu.VMEM((2, 32, 16, 256), BF), pltpu.VMEM((16, 80, 256), F32)],
    )
    corners, features = lax.optimization_barrier((corners, features))
    corners = send(corners, 0, INNER)
    inner, outer = call(
        sides_out_kernel,
        "sides_out",
        [array(side), array(side)],
        [core_s, features, mine, other],
        1.9e9,
        9e6,
        [pltpu.VMEM((2, 32, 16, 256), BF)],
    )
    n, inner = lax.optimization_barrier((n, inner))
    n, s = call(merge_kernel, "merge", [array(strip), array(strip)], [core_s, n, s, corners], 1e6, 2e6)
    n, s, cn, cs, outer, inner = lax.optimization_barrier((n, s, cn, cs, outer, inner))
    inner = send(inner, 0, INNER)
    from_s = send(n, -1, SAME)
    from_n = send(s, 1, SAME)
    outer = send(outer, 0, OUTER)
    corner_s = send(cn, -1, OUTER)
    corner_n = send(cs, 1, OUTER)

    own, hg = call(
        own_kernel,
        "own",
        [array(tile, F32), array(tile, F32)],
        [core_s, features, mine, other, cotangent, proj, conv_bias.reshape(1, 256)],
        1e8,
        12e6,
    )
    hidden, g_top, g_low, gi, go, ct, cl = call(
        point_kernel,
        "point",
        [array(tile), array(strip), array(strip), array(side), array(side), array(small), array(small)],
        [core_s, own, hg, from_n, from_s, inner, outer, corner_n, corner_s],
        1e8,
        6e6,
        [pltpu.VMEM(tile, F32)],
    )

    h_top = send(g_low, 1, SAME)
    h_low = send(g_top, -1, SAME)
    h_outer = send(go, 0, OUTER)
    c_top = send(cl, 1, OUTER)
    c_low = send(ct, -1, OUTER)
    h_inner = send(gi, 0, INNER)

    part = array((3072, 128))
    g_mid, m1, o1 = call(
        wgrad_mid_kernel,
        "wgrad1",
        [array((32, 80, 256)), part, part],
        [core_s, ft, g_top, g_low, h_inner, h_outer],
        1e8,
        6e6,
    )
    r1 = send(o1, 0, INNER)
    hidden, m1 = lax.optimization_barrier((hidden, m1))
    ends = array((64, 8, 128))
    projected, e_mine, e_other = call(
        proj_kernel,
        "proj",
        [array(tile), ends, ends],
        [core_s, hidden, cotangent, proj, g_top, g_low],
        1e8,
        4e6,
        [pltpu.VMEM((256, 256), F32), pltpu.VMEM((64, 8, 128), F32)],
    )
    h_top, h_low, c_top, c_low, e_mine, e_other, m1 = lax.optimization_barrier(
        (h_top, h_low, c_top, c_low, e_mine, e_other, m1)
    )
    (edge,) = call(edge_kernel, "edge", [array(side)], [core_s, h_top, h_low], 1e6, 1e6)
    edge = send(edge, 0, INNER)
    row, long = array((16, 80, 256)), array((3584, 128))
    g_bottom, m0, o0 = call(
        functools.partial(wgrad_row_kernel, 0),
        "wgrad0",
        [row, part, long],
        [core_s, ft, g_mid, h_low, c_low, edge, e_other],
        2.4e9,
        6e6,
    )
    r0 = send(o0, 0, INNER)
    g_upper, m2, o2 = call(
        functools.partial(wgrad_row_kernel, 2),
        "wgrad2",
        [row, part, part],
        [core_s, ft, g_mid, h_top, c_top, edge, e_mine],
        2.4e9,
        6e6,
    )
    r2 = send(o2, 0, INNER)
    (t1,) = call(add_kernel, "add1", [part], [m1, r1], 1e6, 4e6)
    (t0,) = call(add_kernel, "add0", [part], [m0, r0], 1e6, 4e6)
    (total,) = call(
        gather_kernel,
        "gather",
        [array((64, 152, 128))],
        [t0, t1, m2, r2, e_mine, r0],
        1e6,
        7e6,
        [pltpu.VMEM((64, 152, 128), BF), pltpu.SemaphoreType.DMA((8,))],
        limit=49 * 1024 * 1024,
    )
    pieces = lax.all_to_all(total, CHIPS, 0, 0)

    (features_grad,) = call(
        fgrad_kernel, "fgrad", [array((32, 48, 1024))], [g_upper, g_mid, g_bottom, mine, other], 7.2e9, 12e6
    )

    pack = array((80, 128), F32)
    keep, give, bias_row = call(
        sum_kernel,
        "sum",
        [pack, pack, array((1, 128), F32)],
        [core_s, pieces],
        1e6,
        3e6,
        [pltpu.VMEM((152, 128), F32), pltpu.VMEM((64, 152, 128), BF), pltpu.SemaphoreType.DMA((4,))],
        far=(pieces,),
    )
    got = send(give, 0, INNER)
    conv_grad, proj_grad = call(
        join_kernel, "join", [array((72, 256), F32), array((2, 256), F32)], [core_s, keep, got], 1e5, 1e5
    )
    here = 2 * lax.axis_index(ALL) % 128
    bias_grad = lax.dynamic_slice(bias_row.reshape(128), (here,), (2,))
    return projected, features_grad, conv_grad, proj_grad, bias_grad


def solution(mesh):
    fine = Mesh(mesh.devices.reshape(4, 4, 4, 2), ALL)
    tile = P(("y", "x"), ("z", "core"), None)
    rows = P(ALL, None)
    return jax.shard_map(
        body,
        mesh=fine,
        in_specs=(tile, rows, P(), rows, tile),
        out_specs=(tile, tile, rows, rows, P(ALL)),
        check_vma=False,
    )
```
